32 devices in a mesh: row: 4 (over z), col: 8 (over y, x, core).
Axes of the slice: x: 2, y: 2, z: 4, core: 2. Of those that a mesh axis runs over, the one named last changes fastest.
Arguments:
- video_scores_in: float32 [32768, 128], P(('col', 'row')), may hold values from -6 to 6
- audio_seed: int32 [32768], P(('row', 'col')), may hold values from 0 to 255
- video_seed: int32 [32768], P(('col', 'row')), may hold values from 0 to 255
- tile_values: bfloat16 [4, 8, 320, 128, 128], P('row', 'col'), may hold values from 0 to 1
- tile_rows: int32 [4, 8, 320], P('row', 'col'), may hold values from 0 to 63, as said below
- tile_cols: int32 [4, 8, 320], P('row', 'col'), may hold values from 0 to 31, as said below
- tile_count: int32 [4, 8], P('row', 'col'), may hold values from 64 to 320, as said below
Outputs:
- audio_scores: float32 [32768, 128], P(('row', 'col'))
- video_scores: float32 [32768, 128], P(('col', 'row'))
The draws below stay inside these ranges and needn't reach their ends.
Inputs may be any that keep to these rules, and one draw needn't show every extreme that they name: `tile_rows`: every tile row of a cell's row group and every tile column of its column group is named by some live slot of that cell; two slots may name the same tile position, and then both add. `tile_cols`: see tile_rows. `tile_count`: loads differ widely between cells; some cell uses all 320 slots.
All inputs are finite; a program needn't handle non-finite values.
Results may differ from the reference program's by a relative error of at most 0.005.
Values may be sent and summed in bfloat16 or wider, within the bound.
No kernel may reach another device: no remote copies, remote signals or barrier semaphores. Data moves between devices by JAX's collectives and lax.ppermute only.
A program may use at most 192 MiB of HBM per device.

```python
import jax
import jax.numpy as jnp
from jax import lax

CLASSES = 128
TILE = 128
TILE_ROWS = 64
TILE_COLS = 32
TILES_DEV = 320
CLIPS = 32768
N_ROW = 4
N_COL = 8


def tile_layout(key):
    shape_slots = (N_ROW, N_COL, TILES_DEV)
    slot = jnp.arange(TILES_DEV, dtype=jnp.int32)[None, None, :]
    offset_rows = jax.random.randint(jax.random.fold_in(key, 11), (N_ROW, N_COL, 1), 0, TILE_ROWS, dtype=jnp.int32)
    offset_cols = jax.random.randint(jax.random.fold_in(key, 12), (N_ROW, N_COL, 1), 0, TILE_COLS, dtype=jnp.int32)
    random_rows = jax.random.randint(jax.random.fold_in(key, 13), shape_slots, 0, TILE_ROWS, dtype=jnp.int32)
    random_cols = jax.random.randint(jax.random.fold_in(key, 14), shape_slots, 0, TILE_COLS, dtype=jnp.int32)
    covering = slot < TILE_ROWS
    row_ids = jnp.where(covering, (slot + offset_rows) % TILE_ROWS, random_rows)
    col_ids = jnp.where(covering, (slot + offset_cols) % TILE_COLS, random_cols)
    spare = TILES_DEV - TILE_ROWS
    first = jax.random.randint(jax.random.fold_in(key, 15), (N_ROW, N_COL), 0, spare + 1, dtype=jnp.int32)
    second = jax.random.randint(jax.random.fold_in(key, 16), (N_ROW, N_COL), 0, spare + 1, dtype=jnp.int32)
    extra = first * second // spare
    order = jax.random.permutation(jax.random.fold_in(key, 17), N_ROW * N_COL).astype(jnp.int32).reshape(N_ROW, N_COL)
    extra = jnp.where(order == 0, spare, extra)
    return (row_ids, col_ids, TILE_ROWS + extra)


def draw_tile_rows(key, part):
    return tile_layout(key)[0]


def draw_tile_cols(key, part):
    return tile_layout(key)[1]


def draw_tile_count(key, part):
    return tile_layout(key)[2]


def with_ends(result, stream_key, low, high):
    extent = result.shape
    place = [jax.random.randint(jax.random.fold_in(stream_key, axis), (), 0, extent[axis]) for axis in range(len(extent))]
    result = result.at[tuple(place)].set(low)
    longest = extent.index(max(extent))
    place[longest] = (place[longest] + 1) % extent[longest]
    return result.at[tuple(place)].set(high)


def steps_of(own_key, shape, cuts, least, high):
    factor_of, own = 1.0, jax.random.fold_in(own_key, 6)
    for position, blocks in cuts:
        steps = jnp.exp(jax.random.uniform(jax.random.fold_in(own, position), (blocks,), jnp.float32, least / len(cuts), high / len(cuts)))
        factor_of = factor_of * jnp.repeat(steps, shape[position] // blocks).reshape([-1 if axis == position else 1 for axis in range(len(shape))])
    return factor_of


def scatter_about(stream_key, dims, deviation, bound, shards=(), kind=jnp.bfloat16):
    level = steps_of(stream_key, dims, shards, -0.22, 0.18) if shards else 1.0
    entries = jax.random.normal(stream_key, dims, jnp.float32) * deviation * level
    return jnp.minimum(jnp.maximum(entries, -bound), bound).astype(kind)


def setup_inputs(seed: int = 0) -> dict:
    key_list = jax.random.split(jax.random.key(seed), 8)
    video_scores_in = scatter_about(key_list[0], (CLIPS, CLASSES), 1.0, 6.0, ((0, 32),), jnp.float32)
    audio_seed = with_ends(jax.random.randint(key_list[1], (CLIPS,), 0, 2 * CLASSES), jax.random.fold_in(key_list[1], 1), 0, (2 * CLASSES) - 1).astype(jnp.int32)
    video_seed = with_ends(jax.random.randint(key_list[2], (CLIPS,), 0, 2 * CLASSES), jax.random.fold_in(key_list[2], 1), 0, (2 * CLASSES) - 1).astype(jnp.int32)
    tile_values = jnp.clip(1.0 * jax.random.uniform(key_list[3], (N_ROW, N_COL, TILES_DEV, TILE, TILE), jnp.float32) ** steps_of(key_list[3], (N_ROW, N_COL, TILES_DEV, TILE, TILE), ((0, 4), (1, 8)), -0.2, 0.2), 0.0, 1.0).astype(jnp.bfloat16)
    tile_rows = draw_tile_rows(jax.random.fold_in(key_list[7], 71), 0)
    tile_cols = draw_tile_cols(jax.random.fold_in(key_list[7], 71), 0)
    tile_count = draw_tile_count(jax.random.fold_in(key_list[7], 71), 0)
    return dict(video_scores_in=video_scores_in, audio_seed=audio_seed, video_seed=video_seed, tile_values=tile_values, tile_rows=tile_rows, tile_cols=tile_cols, tile_count=tile_count)


blend_weight = 0.75

def blend(total, masses, seed_ids):
    labels = (seed_ids[:, None] == jnp.arange(CLASSES, dtype=jnp.int32)[None, :]).astype(jnp.float32)
    return blend_weight * total / jnp.sqrt(masses)[:, None] + (1.0 - blend_weight) * labels

def reference(video_scores_in, audio_seed, video_seed, tile_values, tile_rows, tile_cols, tile_count):
    cells = N_ROW * N_COL
    flat_vals = tile_values.reshape(cells, TILES_DEV, TILE, TILE)
    flat_rows = tile_rows.reshape(cells, TILES_DEV).astype(jnp.int32)
    flat_cols = tile_cols.reshape(cells, TILES_DEV).astype(jnp.int32)
    flat_count = tile_count.reshape(cells).astype(jnp.int32)
    cell_index = jnp.arange(cells, dtype=jnp.int32)
    row_of = cell_index // N_COL
    col_of = cell_index % N_COL
    slot_index = jnp.arange(TILES_DEV, dtype=jnp.int32)
    video_half = video_scores_in.astype(jnp.bfloat16).reshape(N_COL, TILE_COLS, TILE, CLASSES)

    def forward(state, inputs):
        prop_sum, prop_mass = state
        cell_vals, cell_rows, cell_cols, cell_count, which_row, which_col = inputs
        active_flags = (slot_index < cell_count).astype(jnp.float32)
        panel_tiles = lax.dynamic_index_in_dim(video_half, which_col, 0, keepdims=False)
        selected_entries = jnp.take(panel_tiles, cell_cols, axis=0).astype(jnp.float32)
        edge_weight_list = cell_vals.astype(jnp.float32)
        weighted_products = jnp.einsum('efr,erj->efj', edge_weight_list, selected_entries) * active_flags[:, None, None]
        masses = lax.optimization_barrier(jnp.sum(edge_weight_list, axis=2)) * active_flags[:, None]
        add_sum = jax.ops.segment_sum(weighted_products, cell_rows, num_segments=TILE_ROWS)
        accumulate_mass = jax.ops.segment_sum(masses, cell_rows, num_segments=TILE_ROWS)
        return ((prop_sum.at[which_row].add(add_sum), prop_mass.at[which_row].add(accumulate_mass)), None)
    start = (jnp.zeros((N_ROW, TILE_ROWS, TILE, CLASSES), jnp.float32), jnp.zeros((N_ROW, TILE_ROWS, TILE), jnp.float32))
    (prop_sum, prop_mass), _ = lax.scan(forward, start, (flat_vals, flat_rows, flat_cols, flat_count, row_of, col_of))
    audio_scores = blend(prop_sum.reshape(CLIPS, CLASSES), prop_mass.reshape(CLIPS), audio_seed)
    audio_half = audio_scores.astype(jnp.bfloat16).reshape(N_ROW, TILE_ROWS, TILE, CLASSES)

    def backward(state, inputs):
        back_sum, back_mass = state
        cell_vals, cell_rows, cell_cols, cell_count, which_row, which_col = inputs
        active_flags = (slot_index < cell_count).astype(jnp.float32)
        panel_tiles = lax.dynamic_index_in_dim(audio_half, which_row, 0, keepdims=False)
        selected_entries = jnp.take(panel_tiles, cell_rows, axis=0).astype(jnp.float32)
        edge_weight_list = cell_vals.astype(jnp.float32)
        weighted_products = jnp.einsum('nhv,nhk->nvk', edge_weight_list, selected_entries) * active_flags[:, None, None]
        masses = lax.optimization_barrier(jnp.sum(edge_weight_list, axis=1)) * active_flags[:, None]
        add_sum = jax.ops.segment_sum(weighted_products, cell_cols, num_segments=TILE_COLS)
        accumulate_mass = jax.ops.segment_sum(masses, cell_cols, num_segments=TILE_COLS)
        return ((back_sum.at[which_col].add(add_sum), back_mass.at[which_col].add(accumulate_mass)), None)
    reverse_begin = (jnp.zeros((N_COL, TILE_COLS, TILE, CLASSES), jnp.float32), jnp.zeros((N_COL, TILE_COLS, TILE), jnp.float32))
    (back_sum, back_mass), _ = lax.scan(backward, reverse_begin, (flat_vals, flat_rows, flat_cols, flat_count, row_of, col_of))
    video_scores = blend(back_sum.reshape(CLIPS, CLASSES), back_mass.reshape(CLIPS), video_seed)
    return (audio_scores, video_scores)
```

```python
import functools

import jax
import jax.numpy as jnp
from jax import lax
from jax.experimental import pallas as pl
from jax.experimental.pallas import tpu as pltpu
from jax.sharding import PartitionSpec as P

BLEND = 0.75
CHUNKS = 1
GROUP = 32
VMEM = pl.BlockSpec(memory_space=pltpu.VMEM)
NT = (((1,), (1,)), ((), ()))
NN = (((1,), (0,)), ((), ()))


def params(mib):
    return pltpu.CompilerParams(vmem_limit_bytes=mib * 2**20)


def split_half(mass):
    high = mass.astype(jnp.bfloat16)
    low = (mass - high.astype(jnp.float32)).astype(jnp.bfloat16)
    return jnp.concatenate([high.astype(jnp.float32), low.astype(jnp.float32)], axis=0).astype(
        jnp.bfloat16
    )


def prep_kernel(video_ref, *out_refs):
    tiles = video_ref.shape[0] // 128
    width = out_refs[0].shape[0] // tiles
    for t in range(tiles):
        flipped = video_ref[t * 128 : (t + 1) * 128, :].T.astype(jnp.bfloat16)
        for k, out_ref in enumerate(out_refs):
            out_ref[t * width : (t + 1) * width, :] = flipped[k * width : (k + 1) * width, :]


def prep(video, chunks):
    rows, classes = video.shape
    width = classes // chunks
    shape = jax.ShapeDtypeStruct((rows // 128 * width, 128), jnp.bfloat16)
    return pl.pallas_call(
        prep_kernel, out_shape=[shape] * chunks, in_specs=[VMEM], out_specs=[VMEM] * chunks
    )(video)


def sweep_kernel(
    info, to_ids, from_ids, tiles_ref, *refs, pieces, outs, with_mass, transposed, width, shard
):
    piece_refs = refs[:pieces]
    out_refs = refs[pieces : pieces + outs]
    panel, acc, mass = refs[pieces + outs :]
    step = pl.program_id(0)
    group = tiles_ref.shape[0]
    lhs_rows = width + (16 if with_mass else 0)
    dummy = acc.shape[0] - 1

    @pl.when(step == 0)
    def _():
        for m, piece in enumerate(piece_refs):
            for t in range(shard):
                panel[m * shard + t, :width, :] = piece[t * width : (t + 1) * width, :]
        if with_mass:

            def ones(n, carry):
                panel[n, width:, :] = jnp.ones((16, 128), jnp.bfloat16)
                return carry

            lax.fori_loop(0, panel.shape[0], ones, 0)
            mass[...] = jnp.zeros_like(mass)

        def clear(n, carry):
            acc[n] = jnp.zeros((width, 128), jnp.float32)
            return carry

        lax.fori_loop(0, acc.shape[0], clear, 0)

    live = info[2]

    @pl.when(step * group < live)
    def _():
        for g in range(group):
            slot = step * group + g
            to = jnp.where(slot < live, to_ids[slot] ^ info[0], dummy)
            source = from_ids[slot] ^ info[1]
            product = lax.dot_general(
                panel[source],
                tiles_ref[g],
                NT if transposed else NN,
                preferred_element_type=jnp.float32,
            )
            acc[to] += product[:width]
            if with_mass:
                mass[to] += product[width : width + 8]

    @pl.when(step == pl.num_programs(0) - 1)
    def _():
        per_out = dummy // shard // outs
        for h in range(outs):
            out_ref = out_refs[h]
            for s in range(per_out):
                base = (s * outs + h) * shard
                for t in range(shard):
                    out_ref[s, t * width : (t + 1) * width, :] = acc[base + t].astype(out_ref.dtype)
                if with_mass:
                    own = jnp.concatenate([mass[base + t, 0:1, :] for t in range(shard)], axis=0)
                    out_ref[s, shard * width :, :] = split_half(own)


def sweep(info, to_ids, from_ids, tiles, pieces, to_tiles, outs, with_mass, transposed, width):
    slots = tiles.shape[0]
    shard = pieces[0].shape[0] // width
    group = GROUP
    rows = shard * width + (2 * shard if with_mass else 0)
    lhs_rows = width + (16 if with_mass else 0)
    per_out = to_tiles // shard // outs
    kernel = functools.partial(
        sweep_kernel,
        pieces=len(pieces),
        outs=outs,
        with_mass=with_mass,
        transposed=transposed,
        width=width,
        shard=shard,
    )

    def block(b, info, to_ids, from_ids):
        return (jnp.minimum(b, (info[2] - 1) // group), 0, 0)

    def whole2(b, *_):
        return (0, 0)

    def whole3(b, *_):
        return (0, 0, 0)

    return pl.pallas_call(
        kernel,
        grid_spec=pltpu.PrefetchScalarGridSpec(
            num_scalar_prefetch=3,
            grid=(slots // group,),
            in_specs=[pl.BlockSpec((group, 128, 128), block)]
            + [pl.BlockSpec(p.shape, whole2) for p in pieces],
            out_specs=[pl.BlockSpec((per_out, rows, 128), whole3)] * outs,
            scratch_shapes=[
                pltpu.VMEM((len(pieces) * shard, lhs_rows, 128), jnp.bfloat16),
                pltpu.VMEM((to_tiles + 1, width, 128), jnp.float32),
                pltpu.VMEM((to_tiles + 1, 8, 128), jnp.float32),
            ],
        ),
        out_shape=[jax.ShapeDtypeStruct((per_out, rows, 128), jnp.bfloat16)] * outs,
        compiler_params=params(56),
    )(info, to_ids, from_ids, tiles, *pieces)


def pair_sum_kernel(keep_ref, got_ref, *out_refs, with_mass, body_rows):
    for s, out_ref in enumerate(out_refs):
        total = keep_ref[s, :body_rows].astype(jnp.float32) + got_ref[s, :body_rows].astype(
            jnp.float32
        )
        out_ref[:body_rows, :] = total.astype(out_ref.dtype)
        if with_mass:
            mass = both_halves(keep_ref[s, body_rows:]) + both_halves(got_ref[s, body_rows:])
            if s == 0:
                out_ref[body_rows:, :] = jnp.concatenate([mass, jnp.zeros_like(mass)], axis=0)
            else:
                out_ref[body_rows:, :] = split_half(mass)


def both_halves(block):
    wide = block.astype(jnp.float32)
    half = wide.shape[0] // 2
    return wide[:half] + wide[half:]


def pair_sum(keep, got, with_mass, body_rows):
    count, rows, _ = keep.shape
    shapes = [
        jax.ShapeDtypeStruct((rows, 128), jnp.float32 if s == 0 else jnp.bfloat16)
        for s in range(count)
    ]
    return pl.pallas_call(
        functools.partial(pair_sum_kernel, with_mass=with_mass, body_rows=body_rows),
        out_shape=shapes,
        in_specs=[VMEM] * 2,
        out_specs=[VMEM] * count,
        compiler_params=params(48),
    )(keep, got)


def mix(own, scale, seeds, t, width, first):
    classes = lax.broadcasted_iota(jnp.int32, (width, 128), 0) + first
    labels = jnp.where(classes == seeds[t : t + 1, :], 1.0 - BLEND, 0.0)
    return own * scale[t : t + 1, :] + labels


def audio_kernel(seed_ref, own_ref, *refs, width, shard, first, with_mass):
    refs = list(refs)
    half_ref, full_ref, mass_out = refs[-3:]
    mass_in = None if with_mass else refs[0]
    got = refs[:-3] if with_mass else refs[1:-3]
    body = shard * width
    if with_mass:
        mass = own_ref[body : body + shard, :]
        for g in got:
            mass += both_halves(g[body:])
    else:
        mass = mass_in[...]
    mass_out[...] = mass
    scale = BLEND / jnp.sqrt(mass)
    seeds = seed_ref[...]
    for t in range(shard):
        span = slice(t * width, (t + 1) * width)
        total = own_ref[span, :].astype(jnp.float32)
        for g in got:
            total += g[span, :].astype(jnp.float32)
        scores = mix(total, scale, seeds, t, width, first)
        half_ref[span, :] = scores.astype(jnp.bfloat16)
        full_ref[span, :] = scores


def audio_blend(seeds, own, got, mass, width, first):
    shard = seeds.shape[0]
    args = [seeds, own] + ([] if mass is None else [mass]) + list(got)
    return pl.pallas_call(
        functools.partial(
            audio_kernel, width=width, shard=shard, first=first, with_mass=mass is None
        ),
        out_shape=[
            jax.ShapeDtypeStruct((shard * width, 128), jnp.bfloat16),
            jax.ShapeDtypeStruct((shard * width, 128), jnp.float32),
            jax.ShapeDtypeStruct((shard, 128), jnp.float32),
        ],
        in_specs=[VMEM] * len(args),
        out_specs=[VMEM] * 3,
        compiler_params=params(48),
    )(*args)


def flip_kernel(*refs):
    out_ref = refs[-1]
    width = 128 // (len(refs) - 1)
    for t in range(out_ref.shape[0] // 128):
        parts = [r[t * width : (t + 1) * width, :] for r in refs[:-1]]
        out_ref[t * 128 : (t + 1) * 128, :] = jnp.concatenate(parts, axis=0).T


def flip(parts):
    rows = parts[0].shape[0] * len(parts)
    return pl.pallas_call(
        flip_kernel,
        out_shape=jax.ShapeDtypeStruct((rows, 128), jnp.float32),
        in_specs=[VMEM] * len(parts),
        out_specs=VMEM,
        compiler_params=params(48),
    )(*parts)


def video_kernel(seed_ref, *refs, chunks, width, shard):
    out_ref = refs[-1]
    count = len(refs[:-1]) // chunks
    body = shard * width
    mass = sum(both_halves(r[body:]) for r in refs[:count])
    scale = BLEND / jnp.sqrt(mass)
    seeds = seed_ref[...]
    for t in range(shard):
        span = slice(t * width, (t + 1) * width)
        parts = []
        for k in range(chunks):
            total = refs[k * count][span, :].astype(jnp.float32)
            for r in refs[k * count + 1 : (k + 1) * count]:
                total += r[span, :].astype(jnp.float32)
            parts.append(mix(total, scale, seeds, t, width, k * width))
        out_ref[t * 128 : (t + 1) * 128, :] = jnp.concatenate(parts, axis=0).T


def video_blend(seeds, pieces, width):
    shard = seeds.shape[0]
    flat = [p for chunk in pieces for p in chunk]
    return pl.pallas_call(
        functools.partial(video_kernel, chunks=len(pieces), width=width, shard=shard),
        out_shape=jax.ShapeDtypeStruct((shard * 128, 128), jnp.float32),
        in_specs=[VMEM] * (1 + len(flat)),
        out_specs=VMEM,
        compiler_params=params(48),
    )(seeds, *flat)


def partner(value, axis, mask):
    size = lax.axis_size(axis)
    return lax.ppermute(value, axis, [(i, i ^ mask) for i in range(size)])


def body(video_scores_in, audio_seed, video_seed, tile_values, tile_rows, tile_cols, tile_count):
    tiles = tile_values[0, 0]
    rows, cols = tile_rows[0, 0], tile_cols[0, 0]
    shard = video_scores_in.shape[0] // 128
    chunks, width = CHUNKS, 128 // CHUNKS
    n_row, n_col = lax.axis_size("row"), lax.axis_size("col")
    row_mask = lax.axis_index("row") * shard
    col_mask = lax.axis_index("col") * shard
    live = tile_count[0, 0]
    forward_info = jnp.stack([col_mask, row_mask, live]).astype(jnp.int32)
    reverse_info = jnp.stack([row_mask, col_mask, live]).astype(jnp.int32)
    audio_seeds = audio_seed.reshape(shard, 128)
    video_seeds = video_seed.reshape(shard, 128)

    panels = []
    for own in prep(video_scores_in, chunks):
        panels.append([own] + [partner(own, "row", m) for m in range(1, n_row)])
    halves, fulls, mass = [], [], None
    for k in range(chunks):
        first = k == 0
        keep, send = sweep(
            forward_info, rows, cols, tiles, panels[k], n_col * shard, 2, first, True, width
        )
        got = partner(send, "col", 1)
        own, *others = pair_sum(keep, got, first, shard * width)
        arrived = [partner(x, "col", 2 * (s + 1)) for s, x in enumerate(others)]
        half, full, mass = audio_blend(audio_seeds, own, arrived, mass, width, k * width)
        halves.append(half)
        fulls.append(full)
    results = []
    for k in range(chunks):
        mine = [halves[k]] + [partner(halves[k], "col", m) for m in range(2, n_col, 2)]
        pieces = [q for p in mine for q in (p, partner(p, "col", 1))]
        (sums,) = sweep(
            reverse_info, cols, rows, tiles, pieces, n_row * shard, 1, k == 0, False, width
        )
        results.append([sums[0]] + [partner(sums[m], "row", m) for m in range(1, n_row)])
    return flip(fulls), video_blend(video_seeds, results, width)


def solution(mesh):
    in_specs = (
        P(("col", "row"), None),
        P(("row", "col")),
        P(("col", "row")),
        P("row", "col", None, None, None),
        P("row", "col", None),
        P("row", "col", None),
        P("row", "col"),
    )
    out_specs = (P(("row", "col"), None), P(("col", "row"), None))
    return jax.shard_map(body, mesh=mesh, in_specs=in_specs, out_specs=out_specs, check_vma=False)
```

```python
import functools

import jax
import jax.numpy as jnp
from jax import lax
from jax.experimental import pallas as pl
from jax.experimental.pallas import tpu as pltpu
from jax.sharding import PartitionSpec as P

BLEND = 0.75
GROUP = 16
LIMIT = 40
PLACE = 8
VMEM = pl.BlockSpec(memory_space=pltpu.VMEM)
NT = (((1,), (1,)), ((), ()))
NN = (((1,), (0,)), ((), ()))


def params(mib):
    return pltpu.CompilerParams(vmem_limit_bytes=mib * 2**20)


def split_half(mass):
    high = mass.astype(jnp.bfloat16)
    low = (mass - high.astype(jnp.float32)).astype(jnp.bfloat16)
    return jnp.concatenate([high.astype(jnp.float32), low.astype(jnp.float32)], axis=0).astype(
        jnp.bfloat16
    )


def prep_kernel(video_ref, *out_refs):
    tiles = video_ref.shape[0] // 128
    width = out_refs[0].shape[0] // tiles
    for t in range(tiles):
        flipped = video_ref[t * 128 : (t + 1) * 128, :].T.astype(jnp.bfloat16)
        for k, out_ref in enumerate(out_refs):
            out_ref[t * width : (t + 1) * width, :] = flipped[k * width : (k + 1) * width, :]


def prep(video, chunks):
    rows, classes = video.shape
    width = classes // chunks
    shape = jax.ShapeDtypeStruct((rows // 128 * width, 128), jnp.bfloat16)
    return pl.pallas_call(
        prep_kernel, out_shape=[shape] * chunks, in_specs=[VMEM], out_specs=[VMEM] * chunks
    )(video)


def plan_kernel(rows, cols, live_ref, forward_ref, reverse_ref, counts, *, cap, half, shard):
    row_mask, col_mask = lax.axis_index("row") * shard, lax.axis_index("col") * shard
    live = live_ref[0, 0]
    trash = 2 * cap

    def place(block, carry):
        early, late, far, near = carry
        base = block * PLACE
        found = [(rows[0, 0, base + k], cols[0, 0, base + k]) for k in range(PLACE)]
        for k, (row, col) in enumerate(found):
            slot = base + k
            row, col = row ^ col_mask, col ^ row_mask
            high = (col >= half).astype(jnp.int32)
            local = col - high * half
            there = jnp.where(high == 1, cap + late, early)
            back = jnp.where(high == 1, far, cap + near)
            forward = slot | (local << 12) | (row << 20)
            reverse = slot | (row << 12) | (local << 20)
            used = slot < live
            forward_ref[jnp.where(used, there, trash)] = forward
            reverse_ref[jnp.where(used, back, trash)] = reverse
            low = used.astype(jnp.int32) * (1 - high)
            high = used.astype(jnp.int32) * high
            early, late, far, near = early + low, late + high, far + high, near + low
        return early, late, far, near

    zero = jnp.int32(0)
    blocks = lax.div(live + (PLACE - 1), PLACE)
    early, late, far, near = lax.fori_loop(0, blocks, place, (zero, zero, zero, zero))
    counts[0] = early
    counts[1] = late
    counts[2] = far
    counts[3] = near
    counts[4] = live
    row_dummy = (lax.axis_size("col") * shard) << 20
    col_dummy = half << 20

    def pad(n, carry):
        forward_ref[early + n] = row_dummy
        forward_ref[cap + late + n] = row_dummy
        reverse_ref[far + n] = col_dummy
        reverse_ref[cap + near + n] = col_dummy
        return carry

    lax.fori_loop(0, GROUP, pad, 0)


def plan(rows, cols, live, col_tiles, shard):
    cap = rows.shape[2] + GROUP
    smem = pl.BlockSpec(memory_space=pltpu.SMEM)
    codes = jax.ShapeDtypeStruct((2 * cap + 128,), jnp.int32)
    return pl.pallas_call(
        functools.partial(plan_kernel, cap=cap, half=col_tiles // 2, shard=shard),
        out_shape=[codes, codes, jax.ShapeDtypeStruct((8,), jnp.int32)],
        in_specs=[smem] * 3,
        out_specs=[smem] * 3,
    )(rows, cols, live)


def sweep_kernel(
    codes_ref, counts_ref, tiles_ref, *refs, pieces, carried, kind, outs, first, count_at,
    transposed, shard,
):
    piece_refs = refs[:pieces]
    carry_refs = refs[pieces : pieces + carried]
    out_refs = refs[pieces + carried : pieces + carried + outs]
    codes, counts, panel, acc, mass, slots, code_sem, sems = refs[pieces + carried + outs :]
    width = acc.shape[1]
    dummy = acc.shape[0] - 1
    plans = [
        pltpu.make_async_copy(counts_ref, counts, code_sem.at[0]),
        pltpu.make_async_copy(codes_ref, codes, code_sem.at[1]),
    ]
    for copy in plans:
        copy.start()

    def block(b):
        span = pl.ds(b * GROUP, GROUP)
        return pltpu.make_async_copy(tiles_ref.at[span], slots.at[span], sems.at[b])

    def begin(b, carry):
        block(b).start()
        return carry

    def settle(b, carry):
        block(b).wait()
        return carry

    plans[0].wait()
    blocks = lax.div(counts[4] + (GROUP - 1), GROUP)
    lax.fori_loop(0, blocks, begin, 0)
    for m, piece in enumerate(piece_refs):
        for t in range(shard):
            panel[m * shard + t, :width, :] = piece[t * width : (t + 1) * width, :]

    def ones(n, carry):
        panel[n, width:, :] = jnp.ones((16, 128), jnp.bfloat16)
        return carry

    def clear(n, carry):
        acc[n] = jnp.zeros((width, 128), jnp.float32)
        mass[n] = jnp.zeros((8, 128), jnp.float32)
        return carry

    lax.fori_loop(0, panel.shape[0], ones, 0)
    lax.fori_loop(0, dummy, clear, 0)
    plans[1].wait()
    count = counts[count_at]

    def work(g, settled):
        last = jnp.minimum(g * GROUP + (GROUP - 1), count - 1)
        need = lax.div(codes[first + last] & 0xFFF, GROUP) + 1
        lax.fori_loop(settled, need, settle, 0)
        for k in range(GROUP):
            code = codes[first + g * GROUP + k]
            to = lax.shift_right_logical(code, 20)
            product = lax.dot_general(
                panel[lax.shift_right_logical(code, 12) & 0xFF],
                slots[code & 0xFFF],
                NT if transposed else NN,
                preferred_element_type=jnp.float32,
            )
            acc[to] += product[:width]
            mass[to] += product[width : width + 8]
        return jnp.maximum(settled, need)

    groups = lax.div(count + (GROUP - 1), GROUP)
    settled = lax.fori_loop(0, groups, work, jnp.int32(0))
    lax.fori_loop(settled, blocks, settle, 0)

    if kind == "sums":

        def hand(n, carry):
            out_refs[0][n] = acc[n]
            out_refs[1][n] = mass[n]
            return carry

        lax.fori_loop(0, dummy, hand, 0)
        return
    for n in range(dummy // shard):
        target = out_refs[n] if kind == "each" else out_refs[n % outs].at[n // outs]
        tops = []
        for t in range(shard):
            tile, top = acc[n * shard + t], mass[n * shard + t, 0:1, :]
            if carried:
                tile += carry_refs[0][n * shard + t]
                top += carry_refs[1][n * shard + t, 0:1, :]
            target[t * width : (t + 1) * width, :] = tile.astype(jnp.bfloat16)
            tops.append(top)
        target[shard * width :, :] = split_half(jnp.concatenate(tops, axis=0))


def sweep(
    plan_codes, counts, at, count_at, tiles, pieces, carry, to_tiles, shard, kind, transposed
):
    width = pieces[0].shape[0] // shard
    rows = shard * width + 2 * shard
    shards = to_tiles // shard
    if kind == "sums":
        out_shape = [
            jax.ShapeDtypeStruct((to_tiles, width, 128), jnp.float32),
            jax.ShapeDtypeStruct((to_tiles, 8, 128), jnp.float32),
        ]
    elif kind == "pairs":
        out_shape = [jax.ShapeDtypeStruct((shards // 2, rows, 128), jnp.bfloat16)] * 2
    else:
        out_shape = [jax.ShapeDtypeStruct((rows, 128), jnp.bfloat16)] * shards
    slots = tiles.shape[0]
    average = slots // 4
    any_space = pl.BlockSpec(memory_space=pl.ANY)
    return pl.pallas_call(
        functools.partial(
            sweep_kernel,
            pieces=len(pieces),
            carried=len(carry),
            kind=kind,
            outs=len(out_shape),
            first=at * (slots + GROUP),
            count_at=count_at,
            transposed=transposed,
            shard=shard,
        ),
        in_specs=[any_space] * 3 + [VMEM] * (len(pieces) + len(carry)),
        out_specs=[VMEM] * len(out_shape),
        scratch_shapes=[
            pltpu.SMEM(plan_codes.shape, jnp.int32),
            pltpu.SMEM(counts.shape, jnp.int32),
            pltpu.VMEM((len(pieces) * shard, width + 16, 128), jnp.bfloat16),
            pltpu.VMEM((to_tiles + 1, width, 128), jnp.float32),
            pltpu.VMEM((to_tiles + 1, 8, 128), jnp.float32),
            pltpu.VMEM((slots, 128, 128), jnp.bfloat16),
            pltpu.SemaphoreType.DMA((2,)),
            pltpu.SemaphoreType.DMA((slots // GROUP,)),
        ],
        out_shape=out_shape,
        compiler_params=params(LIMIT),
        cost_estimate=pl.CostEstimate(
            flops=2 * average * 128 * 128 * width * 8,
            bytes_accessed=average * 128 * 128 * 2,
            transcendentals=0,
        ),
    )(plan_codes, counts, tiles, *pieces, *carry)


def pair_sum_kernel(keep_ref, got_ref, *out_refs, body_rows):
    for s in list(range(1, len(out_refs))) + [0]:
        out_ref = out_refs[s]
        total = keep_ref[s, :body_rows].astype(jnp.float32)
        total += got_ref[s, :body_rows].astype(jnp.float32)
        mass = both_halves(keep_ref[s, body_rows:]) + both_halves(got_ref[s, body_rows:])
        out_ref[:body_rows, :] = total.astype(out_ref.dtype)
        if s == 0:
            out_ref[body_rows:, :] = jnp.concatenate([mass, jnp.zeros_like(mass)], axis=0)
        else:
            out_ref[body_rows:, :] = split_half(mass)


def both_halves(block):
    wide = block.astype(jnp.float32)
    half = wide.shape[0] // 2
    return wide[:half] + wide[half:]


def pair_sum(keep, got, body_rows):
    count, rows, _ = keep.shape
    shapes = [
        jax.ShapeDtypeStruct((rows, 128), jnp.float32 if s == 0 else jnp.bfloat16)
        for s in range(count)
    ]
    return pl.pallas_call(
        functools.partial(pair_sum_kernel, body_rows=body_rows),
        out_shape=shapes,
        in_specs=[VMEM] * 2,
        out_specs=[VMEM] * count,
        compiler_params=params(48),
    )(keep, got)


def mix(own, scale, seeds, t, width, first):
    classes = lax.broadcasted_iota(jnp.int32, (width, 128), 0) + first
    labels = jnp.where(classes == seeds[t : t + 1, :], 1.0 - BLEND, 0.0)
    return own * scale[t : t + 1, :] + labels


def audio_kernel(seed_ref, own_ref, *refs, width, shard, first, with_mass):
    refs = list(refs)
    half_ref, full_ref, mass_out = refs[-3:]
    mass_in = None if with_mass else refs[0]
    got = refs[:-3] if with_mass else refs[1:-3]
    body = shard * width
    if with_mass:
        mass = own_ref[body : body + shard, :]
        for g in got:
            mass += both_halves(g[body:])
    else:
        mass = mass_in[...]
    mass_out[...] = mass
    scale = BLEND / jnp.sqrt(mass)
    seeds = seed_ref[...]
    for t in range(shard):
        span = slice(t * width, (t + 1) * width)
        total = own_ref[span, :].astype(jnp.float32)
        for g in got:
            total += g[span, :].astype(jnp.float32)
        scores = mix(total, scale, seeds, t, width, first)
        half_ref[span, :] = scores.astype(jnp.bfloat16)
        full_ref[span, :] = scores


def audio_blend(seeds, own, got, mass, width, first):
    shard = seeds.shape[0]
    args = [seeds, own] + ([] if mass is None else [mass]) + list(got)
    return pl.pallas_call(
        functools.partial(
            audio_kernel, width=width, shard=shard, first=first, with_mass=mass is None
        ),
        out_shape=[
            jax.ShapeDtypeStruct((shard * width, 128), jnp.bfloat16),
            jax.ShapeDtypeStruct((shard * width, 128), jnp.float32),
            jax.ShapeDtypeStruct((shard, 128), jnp.float32),
        ],
        in_specs=[VMEM] * len(args),
        out_specs=[VMEM] * 3,
        compiler_params=params(48),
    )(*args)


def flip_kernel(*refs):
    out_ref = refs[-1]
    width = 128 // (len(refs) - 1)
    for t in range(out_ref.shape[0] // 128):
        parts = [r[t * width : (t + 1) * width, :] for r in refs[:-1]]
        out_ref[t * 128 : (t + 1) * 128, :] = jnp.concatenate(parts, axis=0).T


def flip(parts):
    rows = parts[0].shape[0] * len(parts)
    return pl.pallas_call(
        flip_kernel,
        out_shape=jax.ShapeDtypeStruct((rows, 128), jnp.float32),
        in_specs=[VMEM] * len(parts),
        out_specs=VMEM,
        compiler_params=params(48),
    )(*parts)


def video_kernel(seed_ref, *refs, chunks, width, shard):
    out_ref = refs[-1]
    count = len(refs[:-1]) // chunks
    body = shard * width
    mass = sum(both_halves(r[body:]) for r in refs[:count])
    scale = BLEND / jnp.sqrt(mass)
    seeds = seed_ref[...]
    for t in range(shard):
        span = slice(t * width, (t + 1) * width)
        parts = []
        for k in range(chunks):
            total = refs[k * count][span, :].astype(jnp.float32)
            for r in refs[k * count + 1 : (k + 1) * count]:
                total += r[span, :].astype(jnp.float32)
            parts.append(mix(total, scale, seeds, t, width, k * width))
        out_ref[t * 128 : (t + 1) * 128, :] = jnp.concatenate(parts, axis=0).T


def video_blend(seeds, pieces, width):
    shard = seeds.shape[0]
    flat = [p for chunk in pieces for p in chunk]
    return pl.pallas_call(
        functools.partial(video_kernel, chunks=len(pieces), width=width, shard=shard),
        out_shape=jax.ShapeDtypeStruct((shard * 128, 128), jnp.float32),
        in_specs=[VMEM] * (1 + len(flat)),
        out_specs=VMEM,
        compiler_params=params(48),
    )(seeds, *flat)


def partner(value, axis, mask):
    size = lax.axis_size(axis)
    return lax.ppermute(value, axis, [(i, i ^ mask) for i in range(size)])


def body(video_scores_in, audio_seed, video_seed, tile_values, tile_rows, tile_cols, tile_count):
    tiles = tile_values[0, 0]
    shard, width = video_scores_in.shape[0] // 128, 128
    n_row, n_col = lax.axis_size("row"), lax.axis_size("col")
    row_tiles, col_tiles = n_col * shard, n_row * shard
    audio_seeds = audio_seed.reshape(shard, 128)
    video_seeds = video_seed.reshape(shard, 128)

    (own,) = prep(video_scores_in, 1)
    panel = [own] + [partner(own, "row", m) for m in range(1, n_row)]
    forward, reverse, counts = plan(tile_rows, tile_cols, tile_count, col_tiles, shard)
    near, far = panel[: n_row // 2], panel[n_row // 2 :]
    carry = sweep(
        forward, counts, 0, 0, tiles, near, [], row_tiles, shard, "sums", True
    )
    keep, send = sweep(
        forward, counts, 1, 1, tiles, far, carry, row_tiles, shard, "pairs", True
    )
    got = partner(send, "col", 1)
    own, *others = pair_sum(keep, got, shard * width)
    arrived = [partner(x, "col", 2 * (s + 1)) for s, x in enumerate(others)]
    half, full, _ = audio_blend(audio_seeds, own, arrived, None, width, 0)

    mine = [half] + [partner(half, "col", m) for m in range(2, n_col, 2)]
    pieces = [q for p in mine for q in (p, partner(p, "col", 1))]
    far = sweep(reverse, counts, 0, 2, tiles, pieces, [], col_tiles // 2, shard, "each", False)
    near = sweep(reverse, counts, 1, 3, tiles, pieces, [], col_tiles // 2, shard, "each", False)
    sums = list(near) + list(far)
    results = [sums[0]] + [partner(sums[m], "row", m) for m in range(1, n_row)]
    return flip([full]), video_blend(video_seeds, [results], width)


def solution(mesh):
    in_specs = (
        P(("col", "row"), None),
        P(("row", "col")),
        P(("col", "row")),
        P("row", "col", None, None, None),
        P("row", "col", None),
        P("row", "col", None),
        P("row", "col"),
    )
    out_specs = (P(("row", "col"), None), P(("col", "row"), None))
    return jax.shard_map(body, mesh=mesh, in_specs=in_specs, out_specs=out_specs, check_vma=False)
```

```python
import functools

import jax
import jax.numpy as jnp
from jax import lax
from jax.experimental import pallas as pl
from jax.experimental.pallas import tpu as pltpu
from jax.sharding import PartitionSpec as P

BLEND = 0.75
GROUP = 32
PLACE = 8
NT = (((1,), (1,)), ((), ()))
VMEM = pl.BlockSpec(memory_space=pltpu.VMEM)


def params(mib):
    return pltpu.CompilerParams(vmem_limit_bytes=mib * 2**20)


def split_half(mass):
    high = mass.astype(jnp.bfloat16)
    low = (mass - high.astype(jnp.float32)).astype(jnp.bfloat16)
    return jnp.concatenate([high.astype(jnp.float32), low.astype(jnp.float32)], axis=0).astype(
        jnp.bfloat16
    )


def prep_kernel(video_ref, out_ref):
    out_ref[...] = video_ref[...].astype(jnp.bfloat16)


def prep(video):
    return pl.pallas_call(
        prep_kernel,
        out_shape=jax.ShapeDtypeStruct(video.shape, jnp.bfloat16),
        in_specs=[VMEM],
        out_specs=VMEM,
        compiler_params=params(48),
    )(video)


def plan_kernel(rows, cols, live_ref, _, forward_ref, reverse_ref, counts, *, cap, half, shard):
    row_mask, col_mask = lax.axis_index("row") * shard, lax.axis_index("col") * shard
    live = live_ref[0, 0]
    trash = 2 * cap

    def place(block, carry):
        early, late, far, near = carry
        base = block * PLACE
        found = [(rows[0, 0, base + k], cols[0, 0, base + k]) for k in range(PLACE)]
        for k, (row, col) in enumerate(found):
            slot = base + k
            row, col = row ^ col_mask, col ^ row_mask
            high = (col >= half).astype(jnp.int32)
            local = col - high * half
            there = jnp.where(high == 1, cap + late, early)
            back = jnp.where(high == 1, far, cap + near)
            forward = slot | (local << 12) | (row << 20)
            reverse = slot | (row << 12) | (local << 20)
            used = slot < live
            forward_ref[jnp.where(used, there, trash)] = forward
            reverse_ref[jnp.where(used, back, trash)] = reverse
            low = used.astype(jnp.int32) * (1 - high)
            high = used.astype(jnp.int32) * high
            early, late, far, near = early + low, late + high, far + high, near + low
        return early, late, far, near

    zero = jnp.int32(0)
    blocks = lax.div(live + (PLACE - 1), PLACE)
    early, late, far, near = lax.fori_loop(0, blocks, place, (zero, zero, zero, zero))
    counts[0] = early
    counts[1] = late
    counts[2] = far
    counts[3] = near
    counts[4] = live
    row_dummy = (lax.axis_size("col") * shard) << 20
    col_dummy = half << 20

    def pad(n, carry):
        forward_ref[early + n] = row_dummy
        forward_ref[cap + late + n] = row_dummy
        reverse_ref[far + n] = col_dummy
        reverse_ref[cap + near + n] = col_dummy
        return carry

    lax.fori_loop(0, GROUP, pad, 0)


def plan(rows, cols, live, tiles, col_tiles, shard):
    cap = rows.shape[2] + GROUP
    smem = pl.BlockSpec(memory_space=pltpu.SMEM)
    codes = jax.ShapeDtypeStruct((2 * cap + 128,), jnp.int32)
    return pl.pallas_call(
        functools.partial(plan_kernel, cap=cap, half=col_tiles // 2, shard=shard),
        out_shape=[codes, codes, jax.ShapeDtypeStruct((8,), jnp.int32)],
        in_specs=[smem] * 3 + [VMEM],
        out_specs=[smem] * 3,
        compiler_params=grant(0, [tiles]),
        cost_estimate=pl.CostEstimate(flops=4 * 10**9, bytes_accessed=0, transcendentals=0),
    )(rows, cols, live, tiles)


def fill_panel(panel, piece_refs):
    tiles = piece_refs[0].shape[0] // 128
    for m, piece in enumerate(piece_refs):
        for t in range(tiles):
            panel[m * tiles + t] = piece[t * 128 : (t + 1) * 128, :]


def clear(*sums):
    def one(n, carry):
        for ref in sums:
            ref[n] = jnp.zeros(ref.shape[1:], jnp.float32)
        return carry

    lax.fori_loop(0, sums[0].shape[0] - 1, one, 0)


def groups(count):
    return lax.div(count + (GROUP - 1), GROUP)


def fold_rows(tile):
    return jnp.sum(tile.reshape(16, 8, 128), axis=0)


def early_kernel(codes, counts, tiles_ref, *refs):
    *piece_refs, sums_ref, weights_ref, panel, acc, mass = refs
    dummy = acc.shape[0] - 1
    cap = tiles_ref.shape[0] + GROUP
    fill_panel(panel, piece_refs)
    clear(acc, mass)
    ones = jnp.ones((16, 128), jnp.bfloat16)

    def work(g, carry):
        for k in range(GROUP):
            code = codes[g * GROUP + k]
            part = panel[lax.shift_right_logical(code, 12) & 0xFF]
            acc[lax.shift_right_logical(code, 20)] += jnp.dot(
                tiles_ref[code & 0xFFF], part, preferred_element_type=jnp.float32
            )
        return carry

    lax.fori_loop(0, groups(counts[0]), work, 0)
    for base, at in ((0, 0), (cap, 1)):

        def weigh(g, carry):
            for k in range(GROUP):
                code = codes[base + g * GROUP + k]
                tile = tiles_ref[code & 0xFFF]
                sums = lax.dot_general(ones, tile, NT, preferred_element_type=jnp.float32)
                mass[lax.shift_right_logical(code, 20)] += sums[:8]
            return carry

        lax.fori_loop(0, groups(counts[at]), weigh, 0)

    def hand(n, carry):
        sums_ref[n] = acc[n]
        weights_ref[n] = mass[n]
        return carry

    lax.fori_loop(0, dummy, hand, 0)


def grant(scratch, arrays):
    size = sum(x.size * x.dtype.itemsize for x in arrays)
    return params((scratch + (size if size > 24 * 2**20 else 0)) // 2**20 + 5)


def effort(slots):
    average = slots // 4
    return pl.CostEstimate(
        flops=16 * average * 128**3, bytes_accessed=average * 128 * 256, transcendentals=0
    )


def early_sweep(codes, counts, tiles, pieces, row_tiles):
    smem, slots = pl.BlockSpec(memory_space=pltpu.SMEM), tiles.shape[0]
    out_shape = [
        jax.ShapeDtypeStruct((row_tiles, 128, 128), jnp.float32),
        jax.ShapeDtypeStruct((row_tiles, 8, 128), jnp.float32),
    ]
    scratch = 4 * (row_tiles + 1) * 136 * 128 + sum(p.size for p in pieces) * 2
    return pl.pallas_call(
        early_kernel,
        in_specs=[smem] * 2 + [VMEM] * (1 + len(pieces)),
        out_specs=[VMEM] * 2,
        scratch_shapes=[
            pltpu.VMEM((sum(p.shape[0] for p in pieces) // 128, 128, 128), jnp.bfloat16),
            pltpu.VMEM((row_tiles + 1, 128, 128), jnp.float32),
            pltpu.VMEM((row_tiles + 1, 8, 128), jnp.float32),
        ],
        out_shape=out_shape,
        compiler_params=grant(scratch, [tiles, *pieces, *out_shape]),
        cost_estimate=effort(slots),
    )(codes, counts, tiles, *pieces)


def late_kernel(codes, counts, tiles_ref, sums_ref, weights_ref, *refs, first, at, shard):
    *piece_refs, keep_ref, send_ref, panel, acc = refs
    fill_panel(panel, piece_refs)
    clear(acc)

    def work(g, carry):
        for k in range(GROUP):
            code = codes[first + g * GROUP + k]
            part = panel[lax.shift_right_logical(code, 12) & 0xFF]
            acc[lax.shift_right_logical(code, 20)] += jnp.dot(
                tiles_ref[code & 0xFFF], part, preferred_element_type=jnp.float32
            )
        return carry

    lax.fori_loop(0, groups(counts[at]), work, 0)
    for n in range((acc.shape[0] - 1) // shard):
        target = (keep_ref, send_ref)[n % 2].at[n // 2]
        tops = []
        for t in range(shard):
            tile = acc[n * shard + t] + sums_ref[n * shard + t]
            target[t * 128 : (t + 1) * 128, :] = tile.astype(jnp.bfloat16)
            tops.append(weights_ref[n * shard + t, 0:1, :])
        target[shard * 128 :, :] = split_half(jnp.concatenate(tops, axis=0))


def late_sweep(codes, counts, tiles, sums, weights, pieces, shard):
    smem, slots, row_tiles = pl.BlockSpec(memory_space=pltpu.SMEM), tiles.shape[0], sums.shape[0]
    rows = shard * 130
    out_shape = [jax.ShapeDtypeStruct((row_tiles // shard // 2, rows, 128), jnp.bfloat16)] * 2
    scratch = 4 * (row_tiles + 1) * 128**2 + sum(p.size for p in pieces) * 2
    return pl.pallas_call(
        functools.partial(late_kernel, first=slots + GROUP, at=1, shard=shard),
        in_specs=[smem] * 2 + [VMEM] * (3 + len(pieces)),
        out_specs=[VMEM] * 2,
        scratch_shapes=[
            pltpu.VMEM((sum(p.shape[0] for p in pieces) // 128, 128, 128), jnp.bfloat16),
            pltpu.VMEM((row_tiles + 1, 128, 128), jnp.float32),
        ],
        out_shape=out_shape,
        compiler_params=grant(scratch, [tiles, sums, weights, *pieces, *out_shape]),
        cost_estimate=effort(slots),
    )(codes, counts, tiles, sums, weights, *pieces)


def reverse_kernel(codes, counts, tiles_ref, *refs, pieces, first, at, shard):
    piece_refs, out_refs, (panel, acc, mass) = refs[:pieces], refs[pieces:-3], refs[-3:]
    fill_panel(panel, piece_refs)
    clear(acc, mass)

    def work(g, carry):
        for k in range(GROUP):
            code = codes[first + g * GROUP + k]
            to = lax.shift_right_logical(code, 20)
            tile = tiles_ref[code & 0xFFF]
            part = panel[lax.shift_right_logical(code, 12) & 0xFF]
            acc[to] += jnp.dot(part, tile, preferred_element_type=jnp.float32)
            mass[to] += fold_rows(tile.astype(jnp.float32))
        return carry

    lax.fori_loop(0, groups(counts[at]), work, 0)
    for n, target in enumerate(out_refs):
        tops = []
        for t in range(shard):
            target[t * 128 : (t + 1) * 128, :] = acc[n * shard + t].astype(jnp.bfloat16)
            tops.append(jnp.sum(mass[n * shard + t], axis=0, keepdims=True))
        target[shard * 128 :, :] = split_half(jnp.concatenate(tops, axis=0))


def reverse_sweep(codes, counts, part, tiles, pieces, col_tiles, shard):
    smem, slots = pl.BlockSpec(memory_space=pltpu.SMEM), tiles.shape[0]
    out_shape = [jax.ShapeDtypeStruct((shard * 130, 128), jnp.bfloat16)] * (col_tiles // shard)
    scratch = 4 * (col_tiles + 1) * 136 * 128 + sum(p.size for p in pieces) * 2
    return pl.pallas_call(
        functools.partial(
            reverse_kernel,
            pieces=len(pieces),
            first=part * (slots + GROUP),
            at=2 + part,
            shard=shard,
        ),
        in_specs=[smem] * 2 + [VMEM] * (1 + len(pieces)),
        out_specs=[VMEM] * len(out_shape),
        scratch_shapes=[
            pltpu.VMEM((sum(p.shape[0] for p in pieces) // 128, 128, 128), jnp.bfloat16),
            pltpu.VMEM((col_tiles + 1, 128, 128), jnp.float32),
            pltpu.VMEM((col_tiles + 1, 8, 128), jnp.float32),
        ],
        out_shape=out_shape,
        compiler_params=grant(scratch, [tiles, *pieces, *out_shape]),
        cost_estimate=effort(slots),
    )(codes, counts, tiles, *pieces)


def pair_sum_kernel(keep_ref, got_ref, *out_refs, body_rows):
    for s in list(range(1, len(out_refs))) + [0]:
        out_ref = out_refs[s]
        total = keep_ref[s, :body_rows].astype(jnp.float32)
        total += got_ref[s, :body_rows].astype(jnp.float32)
        mass = both_halves(keep_ref[s, body_rows:]) + both_halves(got_ref[s, body_rows:])
        out_ref[:body_rows, :] = total.astype(out_ref.dtype)
        if s == 0:
            out_ref[body_rows:, :] = jnp.concatenate([mass, jnp.zeros_like(mass)], axis=0)
        else:
            out_ref[body_rows:, :] = split_half(mass)


def both_halves(block):
    wide = block.astype(jnp.float32)
    half = wide.shape[0] // 2
    return wide[:half] + wide[half:]


def pair_sum(keep, got, body_rows):
    count, rows, _ = keep.shape
    shapes = [
        jax.ShapeDtypeStruct((rows, 128), jnp.float32 if s == 0 else jnp.bfloat16)
        for s in range(count)
    ]
    return pl.pallas_call(
        functools.partial(pair_sum_kernel, body_rows=body_rows),
        out_shape=shapes,
        in_specs=[VMEM] * 2,
        out_specs=[VMEM] * count,
        compiler_params=params(48),
    )(keep, got)


def spread(row):
    return jnp.broadcast_to(row, (128, 128))


def audio_kernel(label_ref, own_ref, *refs, shard):
    got, (half_ref, full_ref) = refs[:-2], refs[-2:]
    body = shard * 128
    mass = own_ref[body : body + shard, :]
    for g in got:
        mass += both_halves(g[body:])
    scale = BLEND / jnp.sqrt(mass)
    for t in range(shard):
        span = slice(t * 128, (t + 1) * 128)
        total = own_ref[span, :]
        for g in got:
            total += g[span, :].astype(jnp.float32)
        scores = total * spread(scale[t : t + 1, :]).T + label_ref[span, :]
        full_ref[span, :] = scores
        half_ref[span, :] = scores.T.astype(jnp.bfloat16)


def audio_blend(labels, own, got):
    shard = labels.shape[0] // 128
    shape = (shard * 128, 128)
    return pl.pallas_call(
        functools.partial(audio_kernel, shard=shard),
        out_shape=[
            jax.ShapeDtypeStruct(shape, jnp.bfloat16),
            jax.ShapeDtypeStruct(shape, jnp.float32),
        ],
        in_specs=[VMEM] * (2 + len(got)),
        out_specs=[VMEM] * 2,
        compiler_params=params(48),
    )(labels, own, *got)


def video_kernel(seed_ref, *refs, shard):
    got, out_ref = refs[:-1], refs[-1]
    body = shard * 128
    scale = BLEND / jnp.sqrt(sum(both_halves(r[body:]) for r in got))
    seeds = seed_ref[...]
    classes = lax.broadcasted_iota(jnp.int32, (128, 128), 0)
    for t in range(shard):
        span = slice(t * 128, (t + 1) * 128)
        total = sum(r[span, :].astype(jnp.float32) for r in got)
        labels = jnp.where(classes == seeds[t : t + 1, :], 1.0 - BLEND, 0.0)
        out_ref[span, :] = (total * scale[t : t + 1, :] + labels).T


def video_blend(seeds, pieces):
    shard = seeds.shape[0]
    return pl.pallas_call(
        functools.partial(video_kernel, shard=shard),
        out_shape=jax.ShapeDtypeStruct((shard * 128, 128), jnp.float32),
        in_specs=[VMEM] * (1 + len(pieces)),
        out_specs=VMEM,
        compiler_params=params(48),
    )(seeds, *pieces)


def partner(value, axis, mask):
    size = lax.axis_size(axis)
    return lax.ppermute(value, axis, [(i, i ^ mask) for i in range(size)])


def body(video_scores_in, audio_seed, video_seed, tile_values, tile_rows, tile_cols, tile_count):
    tiles = tile_values[0, 0]
    shard = video_scores_in.shape[0] // 128
    n_row, n_col = lax.axis_size("row"), lax.axis_size("col")
    row_tiles, col_tiles = n_col * shard, n_row * shard
    classes = jnp.arange(128, dtype=jnp.int32)[None, :]
    labels = jnp.where(audio_seed[:, None] == classes, jnp.float32(1.0 - BLEND), jnp.float32(0.0))
    video_seeds = video_seed.reshape(shard, 128)

    own = prep(video_scores_in)
    panel = [own] + [partner(own, "row", m) for m in range(1, n_row)]
    forward, reverse, counts = plan(tile_rows, tile_cols, tile_count, tiles, col_tiles, shard)
    near, far = panel[: n_row // 2], panel[n_row // 2 :]
    sums, weights = early_sweep(forward, counts, tiles, near, row_tiles)
    keep, send = late_sweep(forward, counts, tiles, sums, weights, far, shard)
    got = partner(send, "col", 1)
    own, *others = pair_sum(keep, got, shard * 128)
    arrived = [partner(x, "col", 2 * (s + 1)) for s, x in enumerate(others)]
    half, audio_scores = audio_blend(labels, own, arrived)

    mine = [half] + [partner(half, "col", m) for m in range(2, n_col, 2)]
    pieces = [q for p in mine for q in (p, partner(p, "col", 1))]
    far = reverse_sweep(reverse, counts, 0, tiles, pieces, col_tiles // 2, shard)
    near = reverse_sweep(reverse, counts, 1, tiles, pieces, col_tiles // 2, shard)
    sums = list(near) + list(far)
    results = [sums[0]] + [partner(sums[m], "row", m) for m in range(1, n_row)]
    return audio_scores, video_blend(video_seeds, results)


def solution(mesh):
    in_specs = (
        P(("col", "row"), None),
        P(("row", "col")),
        P(("col", "row")),
        P("row", "col", None, None, None),
        P("row", "col", None),
        P("row", "col", None),
        P("row", "col"),
    )
    out_specs = (P(("row", "col"), None), P(("col", "row"), None))
    return jax.shard_map(body, mesh=mesh, in_specs=in_specs, out_specs=out_specs, check_vma=False)
```

```python
import functools

import jax
import jax.numpy as jnp
from jax import lax
from jax.experimental import pallas as pl
from jax.experimental.pallas import tpu as pltpu
from jax.sharding import PartitionSpec as P

BLEND = 0.75
GROUP = 32
PLACE = 8
NT = (((1,), (1,)), ((), ()))
VMEM = pl.BlockSpec(memory_space=pltpu.VMEM)


def params(mib):
    return pltpu.CompilerParams(vmem_limit_bytes=mib * 2**20)


def split_half(mass):
    high = mass.astype(jnp.bfloat16)
    low = (mass - high.astype(jnp.float32)).astype(jnp.bfloat16)
    return jnp.concatenate([high.astype(jnp.float32), low.astype(jnp.float32)], axis=0).astype(
        jnp.bfloat16
    )


def prep_kernel(video_ref, out_ref):
    out_ref[...] = video_ref[...].astype(jnp.bfloat16)


def prep(video):
    return pl.pallas_call(
        prep_kernel,
        out_shape=jax.ShapeDtypeStruct(video.shape, jnp.bfloat16),
        in_specs=[VMEM],
        out_specs=VMEM,
        compiler_params=params(48),
    )(video)


def plan_kernel(rows, cols, live_ref, _, codes_ref, counts, *, cap, half, shard):
    row_mask, col_mask = lax.axis_index("row") * shard, lax.axis_index("col") * shard
    live = live_ref[0, 0]
    trash = 3 * cap

    def place(block, carry):
        own, near, far = carry
        base = block * PLACE
        found = [(rows[0, 0, base + k], cols[0, 0, base + k]) for k in range(PLACE)]
        for k, (row, col) in enumerate(found):
            slot = base + k
            row, col = row ^ col_mask, col ^ row_mask
            is_far = col >= half
            is_own = col < shard
            spot = jnp.where(is_far, 2 * cap + far, jnp.where(is_own, own, cap + near))
            codes_ref[jnp.where(slot < live, spot, trash)] = slot | (col << 12) | (row << 20)
            one = (slot < live).astype(jnp.int32)
            near += jnp.where(is_far | is_own, 0, one)
            own += jnp.where(is_own, one, 0)
            far += jnp.where(is_far, one, 0)
        return own, near, far

    zero = jnp.int32(0)
    found = lax.fori_loop(0, lax.div(live + (PLACE - 1), PLACE), place, (zero, zero, zero))
    row_dummy = (lax.axis_size("col") * shard) << 20
    for n, count in enumerate(found):
        counts[n] = count
    for n, count in enumerate(found):
        dummy = row_dummy | ((half if n < 2 else 2 * half) << 12)

        def pad(k, carry):
            codes_ref[n * cap + count + k] = dummy
            return carry

        lax.fori_loop(0, GROUP, pad, 0)


def plan(rows, cols, live, tiles, col_tiles, shard):
    cap = rows.shape[2] + GROUP
    smem = pl.BlockSpec(memory_space=pltpu.SMEM)
    return pl.pallas_call(
        functools.partial(plan_kernel, cap=cap, half=col_tiles // 2, shard=shard),
        out_shape=[
            jax.ShapeDtypeStruct((3 * cap + 128,), jnp.int32),
            jax.ShapeDtypeStruct((3,), jnp.int32),
        ],
        in_specs=[smem] * 3 + [VMEM],
        out_specs=[smem] * 2,
        compiler_params=grant(0, [tiles]),
    )(rows, cols, live, tiles)


def walk(codes, counts, lists, visit):
    cap = (codes.shape[0] - 128) // 3
    for n in lists:

        def group(g, carry):
            for k in range(GROUP):
                code = codes[n * cap + g * GROUP + k]
                col = lax.shift_right_logical(code, 12) & 0xFF
                visit(code & 0xFFF, col, lax.shift_right_logical(code, 20))
            return carry

        lax.fori_loop(0, lax.div(counts[n] + (GROUP - 1), GROUP), group, 0)


def fill_panel(panel, piece_refs):
    tiles = piece_refs[0].shape[0] // 128
    for m, piece in enumerate(piece_refs):
        for t in range(tiles):
            panel[m * tiles + t] = piece[t * 128 : (t + 1) * 128, :]


def clear(*sums):
    def one(n, carry):
        for ref in sums:
            ref[n] = jnp.zeros(ref.shape[1:], jnp.float32)
        return carry

    lax.fori_loop(0, sums[0].shape[0] - 1, one, 0)


def fold_rows(tile):
    return jnp.sum(tile.reshape(16, 8, 128), axis=0)


def early_kernel(codes, counts, tiles_ref, *refs):
    *piece_refs, sums_ref, weights_ref, panel, acc, mass = refs
    fill_panel(panel, piece_refs)
    clear(acc, mass)
    ones = jnp.ones((16, 128), jnp.bfloat16)

    def multiply(slot, col, row):
        part = panel[col & (panel.shape[0] - 1)]
        acc[row] += jnp.dot(tiles_ref[slot], part, preferred_element_type=jnp.float32)

    def weigh(slot, col, row):
        sums = lax.dot_general(ones, tiles_ref[slot], NT, preferred_element_type=jnp.float32)
        mass[row] += sums[:8]

    walk(codes, counts, [0], multiply)
    walk(codes, counts, [0, 1, 2], weigh)

    def hand(n, carry):
        sums_ref[n] = acc[n]
        weights_ref[n] = mass[n]
        return carry

    lax.fori_loop(0, acc.shape[0] - 1, hand, 0)


def grant(scratch, arrays):
    size = sum(x.size * x.dtype.itemsize for x in arrays)
    return params((scratch + (size if size > 24 * 2**20 else 0)) // 2**20 + 5)


def effort(slots):
    average = slots // 4
    return pl.CostEstimate(
        flops=16 * average * 128**3, bytes_accessed=average * 128 * 256, transcendentals=0
    )


def early_sweep(codes, counts, tiles, pieces, row_tiles):
    smem, slots = pl.BlockSpec(memory_space=pltpu.SMEM), tiles.shape[0]
    out_shape = [
        jax.ShapeDtypeStruct((row_tiles, 128, 128), jnp.float32),
        jax.ShapeDtypeStruct((row_tiles, 8, 128), jnp.float32),
    ]
    scratch = 4 * (row_tiles + 1) * 136 * 128 + sum(p.size for p in pieces) * 2
    return pl.pallas_call(
        early_kernel,
        in_specs=[smem] * 2 + [VMEM] * (1 + len(pieces)),
        out_specs=[VMEM] * 2,
        scratch_shapes=[
            pltpu.VMEM((sum(p.shape[0] for p in pieces) // 128, 128, 128), jnp.bfloat16),
            pltpu.VMEM((row_tiles + 1, 128, 128), jnp.float32),
            pltpu.VMEM((row_tiles + 1, 8, 128), jnp.float32),
        ],
        out_shape=out_shape,
        compiler_params=grant(scratch, [tiles, *pieces, *out_shape]),
        cost_estimate=effort(slots),
    )(codes, counts, tiles, *pieces)


def late_kernel(codes, counts, tiles_ref, sums_ref, weights_ref, *refs, shard):
    count_out = sums_ref.shape[0] // shard
    piece_refs, out_refs, (panel, acc) = refs[: -2 - count_out], refs[-2 - count_out : -2], refs[-2:]
    fill_panel(panel.at[pl.ds(shard, panel.shape[0] - shard)], piece_refs)
    panel[0] = jnp.zeros((128, 128), jnp.bfloat16)

    def begin(n, carry):
        acc[n] = sums_ref[n]
        return carry

    lax.fori_loop(0, sums_ref.shape[0], begin, 0)

    def multiply(slot, col, row):
        part = panel[col & (panel.shape[0] - 1)]
        acc[row] += jnp.dot(tiles_ref[slot], part, preferred_element_type=jnp.float32)

    walk(codes, counts, [1, 2], multiply)
    for n, target in enumerate(out_refs):
        tops = []
        for t in range(shard):
            target[t * 128 : (t + 1) * 128, :] = acc[n * shard + t].astype(jnp.bfloat16)
            tops.append(weights_ref[n * shard + t, 0:1, :])
        target[shard * 128 :, :] = split_half(jnp.concatenate(tops, axis=0))


def late_sweep(codes, counts, tiles, sums, weights, pieces, shard):
    smem, slots, row_tiles = pl.BlockSpec(memory_space=pltpu.SMEM), tiles.shape[0], sums.shape[0]
    rows = shard * 130
    out_shape = [jax.ShapeDtypeStruct((rows, 128), jnp.bfloat16)] * (row_tiles // shard)
    scratch = 4 * (row_tiles + 1) * 128**2 + sum(p.size for p in pieces) * 2
    return pl.pallas_call(
        functools.partial(late_kernel, shard=shard),
        in_specs=[smem] * 2 + [VMEM] * (3 + len(pieces)),
        out_specs=[VMEM] * len(out_shape),
        scratch_shapes=[
            pltpu.VMEM((shard + sum(p.shape[0] for p in pieces) // 128, 128, 128), jnp.bfloat16),
            pltpu.VMEM((row_tiles + 1, 128, 128), jnp.float32),
        ],
        out_shape=out_shape,
        compiler_params=grant(scratch, [tiles, sums, weights, *pieces, *out_shape]),
        cost_estimate=effort(slots),
    )(codes, counts, tiles, sums, weights, *pieces)


def reverse_kernel(codes, counts, tiles_ref, *refs, pieces, lists, first, shard):
    piece_refs, out_refs, (panel, acc, mass) = refs[:pieces][::-1], refs[pieces:-3], refs[-3:]
    fill_panel(panel, piece_refs)
    clear(acc, mass)

    def multiply(slot, col, row):
        tile, part = tiles_ref[slot], panel[row & (panel.shape[0] - 1)]
        acc[col - first] += jnp.dot(part, tile, preferred_element_type=jnp.float32)
        mass[col - first] += fold_rows(tile.astype(jnp.float32))

    walk(codes, counts, lists, multiply)
    for n, target in enumerate(out_refs):
        tops = []
        for t in range(shard):
            target[t * 128 : (t + 1) * 128, :] = acc[n * shard + t].astype(jnp.bfloat16)
            tops.append(jnp.sum(mass[n * shard + t], axis=0, keepdims=True))
        target[shard * 128 :, :] = split_half(jnp.concatenate(tops, axis=0))


def reverse_sweep(codes, counts, lists, first, tiles, pieces, col_tiles, shard):
    smem, slots = pl.BlockSpec(memory_space=pltpu.SMEM), tiles.shape[0]
    out_shape = [jax.ShapeDtypeStruct((shard * 130, 128), jnp.bfloat16)] * (col_tiles // shard)
    scratch = 4 * (col_tiles + 1) * 136 * 128 + sum(p.size for p in pieces) * 2
    return pl.pallas_call(
        functools.partial(
            reverse_kernel,
            pieces=len(pieces),
            lists=lists,
            first=first,
            shard=shard,
        ),
        in_specs=[smem] * 2 + [VMEM] * (1 + len(pieces)),
        out_specs=[VMEM] * len(out_shape),
        scratch_shapes=[
            pltpu.VMEM((sum(p.shape[0] for p in pieces) // 128, 128, 128), jnp.bfloat16),
            pltpu.VMEM((col_tiles + 1, 128, 128), jnp.float32),
            pltpu.VMEM((col_tiles + 1, 8, 128), jnp.float32),
        ],
        out_shape=out_shape,
        compiler_params=grant(scratch, [tiles, *pieces, *out_shape]),
        cost_estimate=effort(slots),
    )(codes, counts, tiles, *pieces)


def pair_sum_kernel(keep_ref, got_ref, out_ref, *, body_rows):
    total = keep_ref[:body_rows].astype(jnp.float32) + got_ref[:body_rows].astype(jnp.float32)
    out_ref[:body_rows, :] = total.astype(out_ref.dtype)
    mass = both_halves(keep_ref[body_rows:]) + both_halves(got_ref[body_rows:])
    if out_ref.dtype == jnp.float32:
        out_ref[body_rows:, :] = jnp.concatenate([mass, jnp.zeros_like(mass)], axis=0)
    else:
        out_ref[body_rows:, :] = split_half(mass)


def both_halves(block):
    wide = block.astype(jnp.float32)
    half = wide.shape[0] // 2
    return wide[:half] + wide[half:]


def pair_sum(keep, got, body_rows, kind):
    return pl.pallas_call(
        functools.partial(pair_sum_kernel, body_rows=body_rows),
        out_shape=jax.ShapeDtypeStruct(keep.shape, kind),
        in_specs=[VMEM] * 2,
        out_specs=VMEM,
        compiler_params=params(48),
    )(keep, got)


def mix(total, scale, seeds, t):
    classes = lax.broadcasted_iota(jnp.int32, (128, 128), 0)
    labels = jnp.where(classes == seeds[t : t + 1, :], 1.0 - BLEND, 0.0)
    return total * scale[t : t + 1, :] + labels


def audio_kernel(seed_ref, own_ref, *refs, shard):
    got, (half_ref, turned_ref) = refs[:-2], refs[-2:]
    body = shard * 128
    mass = own_ref[body : body + shard, :]
    for g in got:
        mass += both_halves(g[body:])
    scale = BLEND / jnp.sqrt(mass)
    seeds = seed_ref[...]
    for t in range(shard):
        span = slice(t * 128, (t + 1) * 128)
        total = own_ref[span, :]
        for g in got:
            total += g[span, :].astype(jnp.float32)
        scores = mix(total.T, scale, seeds, t)
        turned_ref[span, :] = scores
        half_ref[span, :] = scores.astype(jnp.bfloat16)


def audio_blend(seeds, own, got):
    shard = seeds.shape[0]
    shape = (shard * 128, 128)
    return pl.pallas_call(
        functools.partial(audio_kernel, shard=shard),
        out_shape=[
            jax.ShapeDtypeStruct(shape, jnp.bfloat16),
            jax.ShapeDtypeStruct(shape, jnp.float32),
        ],
        in_specs=[VMEM] * (2 + len(got)),
        out_specs=[VMEM] * 2,
        compiler_params=params(48),
    )(seeds, own, *got)


def flip_kernel(turned_ref, out_ref):
    for t in range(out_ref.shape[0] // 128):
        span = slice(t * 128, (t + 1) * 128)
        out_ref[span, :] = turned_ref[span, :].T


def flip(turned):
    return pl.pallas_call(
        flip_kernel,
        out_shape=jax.ShapeDtypeStruct(turned.shape, jnp.float32),
        in_specs=[VMEM],
        out_specs=VMEM,
        compiler_params=params(48),
    )(turned)


def video_kernel(seed_ref, *refs, shard):
    got, out_ref = refs[:-1], refs[-1]
    body = shard * 128
    scale = BLEND / jnp.sqrt(sum(both_halves(r[body:]) for r in got))
    seeds = seed_ref[...]
    for t in range(shard):
        span = slice(t * 128, (t + 1) * 128)
        total = sum(r[span, :].astype(jnp.float32) for r in got)
        out_ref[span, :] = mix(total, scale, seeds, t).T


def video_blend(seeds, pieces):
    shard = seeds.shape[0]
    return pl.pallas_call(
        functools.partial(video_kernel, shard=shard),
        out_shape=jax.ShapeDtypeStruct((shard * 128, 128), jnp.float32),
        in_specs=[VMEM] * (1 + len(pieces)),
        out_specs=VMEM,
        compiler_params=params(48),
    )(seeds, *pieces)


def partner(value, axis, mask):
    size = lax.axis_size(axis)
    return lax.ppermute(value, axis, [(i, i ^ mask) for i in range(size)])


def body(video_scores_in, audio_seed, video_seed, tile_values, tile_rows, tile_cols, tile_count):
    tiles = tile_values[0, 0]
    shard = video_scores_in.shape[0] // 128
    n_row, n_col = lax.axis_size("row"), lax.axis_size("col")
    row_tiles, col_tiles = n_col * shard, n_row * shard
    audio_seeds = audio_seed.reshape(shard, 128)
    video_seeds = video_seed.reshape(shard, 128)

    own = prep(video_scores_in)
    others = [partner(own, "row", m) for m in range(1, n_row)]
    codes, counts = plan(tile_rows, tile_cols, tile_count, tiles, col_tiles, shard)
    sums, weights = early_sweep(codes, counts, tiles, [own], row_tiles)
    payloads = late_sweep(codes, counts, tiles, sums, weights, others, shard)
    owned = {}
    for n in [*range(2, n_col, 2), 0]:
        kind = jnp.bfloat16 if n else jnp.float32
        got = partner(payloads[n + 1], "col", 1)
        owned[n] = pair_sum(payloads[n], got, shard * 128, kind)
    arrived = [partner(owned[n], "col", n) for n in range(2, n_col, 2)]
    half, turned = audio_blend(audio_seeds, owned[0], arrived)

    mine = [half] + [partner(half, "col", m) for m in range(2, n_col, 2)]
    pieces = [q for p in mine for q in (p, partner(p, "col", 1))]
    half_tiles = col_tiles // 2
    pieces = pieces[::-1]
    far = reverse_sweep(codes, counts, [2], half_tiles, tiles, pieces, half_tiles, shard)
    near = reverse_sweep(codes, counts, [0, 1], 0, tiles, pieces, half_tiles, shard)
    sums = list(near) + list(far)
    results = [sums[0]] + [partner(sums[m], "row", m) for m in range(1, n_row)]
    return flip(turned), video_blend(video_seeds, results)


def solution(mesh):
    in_specs = (
        P(("col", "row"), None),
        P(("row", "col")),
        P(("col", "row")),
        P("row", "col", None, None, None),
        P("row", "col", None),
        P("row", "col", None),
        P("row", "col"),
    )
    out_specs = (P(("row", "col"), None), P(("col", "row"), None))
    return jax.shard_map(body, mesh=mesh, in_specs=in_specs, out_specs=out_specs, check_vma=False)
```

```python
import functools

import jax
import jax.numpy as jnp
from jax import lax
from jax.experimental import pallas as pl
from jax.experimental.pallas import tpu as pltpu
from jax.sharding import PartitionSpec as P

BLEND = 0.75
GROUP = 32
PLACE = 8
VMEM = pl.BlockSpec(memory_space=pltpu.VMEM)


def params(mib):
    return pltpu.CompilerParams(vmem_limit_bytes=mib * 2**20)


def split_half(mass):
    high = mass.astype(jnp.bfloat16)
    low = (mass - high.astype(jnp.float32)).astype(jnp.bfloat16)
    return jnp.concatenate([high.astype(jnp.float32), low.astype(jnp.float32)], axis=0).astype(
        jnp.bfloat16
    )


def prep_kernel(video_ref, out_ref):
    out_ref[...] = video_ref[...].astype(jnp.bfloat16)


def prep(video):
    return pl.pallas_call(
        prep_kernel,
        out_shape=jax.ShapeDtypeStruct(video.shape, jnp.bfloat16),
        in_specs=[VMEM],
        out_specs=VMEM,
        compiler_params=params(48),
    )(video)


def plan_kernel(rows, cols, live_ref, _, codes_ref, counts, *, cap, half, shard):
    row_mask, col_mask = lax.axis_index("row") * shard, lax.axis_index("col") * shard
    live = live_ref[0, 0]
    for n in range(4):
        counts[n] = 0

    def place(block, carry):
        base = block * PLACE
        found = [(rows[0, 0, base + k], cols[0, 0, base + k]) for k in range(PLACE)]
        for k, (row, col) in enumerate(found):
            slot = base + k
            row, col = row ^ col_mask, col ^ row_mask
            region = (col >= shard).astype(jnp.int32) + (col >= half).astype(jnp.int32)
            region = jnp.where(slot < live, region, 3)
            count = counts[region]
            codes_ref[region * cap + count] = slot | (col << 12) | (row << 20)
            counts[region] = count + 1
        return carry

    lax.fori_loop(0, lax.div(live + (PLACE - 1), PLACE), place, 0)
    found = [counts[n] for n in range(3)]
    row_dummy = (lax.axis_size("col") * shard) << 20
    for n, count in enumerate(found):
        dummy = row_dummy | ((half if n < 2 else 2 * half) << 12)

        def pad(k, carry):
            codes_ref[n * cap + count + k] = dummy
            return carry

        lax.fori_loop(0, GROUP, pad, 0)


def plan(rows, cols, live, tiles, col_tiles, shard):
    cap = rows.shape[2] + GROUP
    smem = pl.BlockSpec(memory_space=pltpu.SMEM)
    return pl.pallas_call(
        functools.partial(plan_kernel, cap=cap, half=col_tiles // 2, shard=shard),
        out_shape=[
            jax.ShapeDtypeStruct((3 * cap + 128,), jnp.int32),
            jax.ShapeDtypeStruct((4,), jnp.int32),
        ],
        in_specs=[smem] * 3 + [VMEM],
        out_specs=[smem] * 2,
        compiler_params=grant(0, [tiles]),
    )(rows, cols, live, tiles)


def walk(codes, counts, lists, visit):
    cap = (codes.shape[0] - 128) // 3
    for n in lists:

        def group(g, carry):
            for k in range(GROUP):
                code = codes[n * cap + g * GROUP + k]
                col = lax.shift_right_logical(code, 12) & 0xFF
                visit(code & 0xFFF, col, lax.shift_right_logical(code, 20))
            return carry

        lax.fori_loop(0, lax.div(counts[n] + (GROUP - 1), GROUP), group, 0)


def fill_panel(panel, piece_refs):
    tiles = piece_refs[0].shape[0] // 128
    for m, piece in enumerate(piece_refs):
        for t in range(tiles):
            panel[m * tiles + t] = piece[t * 128 : (t + 1) * 128, :]


def clear(*sums):
    def one(n, carry):
        for ref in sums:
            ref[n] = jnp.zeros(ref.shape[1:], jnp.float32)
        return carry

    lax.fori_loop(0, sums[0].shape[0] - 1, one, 0)


def fold_rows(tile):
    return jnp.sum(tile.reshape(16, 8, 128), axis=0)


def early_kernel(codes, counts, tiles_ref, own_ref, sums_ref, weights_ref, panel, mass):
    fill_panel(panel, [own_ref])
    clear(mass)
    ones = jnp.ones((128, 128), jnp.bfloat16)

    def begin(n, carry):
        sums_ref[n] = jnp.zeros((128, 128), jnp.float32)
        return carry

    def multiply(slot, col, row):
        part = panel[col & (panel.shape[0] - 1)]
        sums_ref[row] += jnp.dot(tiles_ref[slot], part, preferred_element_type=jnp.float32)

    def weigh(slot, col, row):
        mass[row] += jnp.dot(tiles_ref[slot], ones, preferred_element_type=jnp.float32)

    lax.fori_loop(0, sums_ref.shape[0], begin, 0)
    walk(codes, counts, [0], multiply)
    walk(codes, counts, [0, 1, 2], weigh)

    diagonal = lax.broadcasted_iota(jnp.int32, (128, 128), 0) == lax.broadcasted_iota(
        jnp.int32, (128, 128), 1
    )

    def hand(n, carry):
        weights_ref[n] = fold_rows(jnp.where(diagonal, mass[n], 0.0))
        return carry

    lax.fori_loop(0, weights_ref.shape[0], hand, 0)


def middle_kernel(codes, counts, tiles_ref, sums_ref, *refs, shard):
    *piece_refs, out_ref, panel = refs
    fill_panel(panel.at[pl.ds(shard, panel.shape[0] - shard)], piece_refs)
    panel[0] = jnp.zeros((128, 128), jnp.bfloat16)

    def begin(n, carry):
        out_ref[n] = sums_ref[n]
        return carry

    def multiply(slot, col, row):
        part = panel[col & (panel.shape[0] - 1)]
        out_ref[row] += jnp.dot(tiles_ref[slot], part, preferred_element_type=jnp.float32)

    lax.fori_loop(0, sums_ref.shape[0], begin, 0)
    walk(codes, counts, [1], multiply)


def grant(scratch, arrays):
    size = sum(x.size * x.dtype.itemsize for x in arrays)
    return params((scratch + (size if size > 24 * 2**20 else 0)) // 2**20 + 5)


def effort(slots):
    average = slots // 4
    return pl.CostEstimate(
        flops=16 * average * 128**3, bytes_accessed=average * 128 * 256, transcendentals=0
    )


def early_sweep(codes, counts, tiles, own, row_tiles):
    smem, slots = pl.BlockSpec(memory_space=pltpu.SMEM), tiles.shape[0]
    out_shape = [
        jax.ShapeDtypeStruct((row_tiles + 1, 128, 128), jnp.float32),
        jax.ShapeDtypeStruct((row_tiles, 8, 128), jnp.float32),
    ]
    return pl.pallas_call(
        early_kernel,
        in_specs=[smem] * 2 + [VMEM] * 2,
        out_specs=[VMEM] * 2,
        scratch_shapes=[
            pltpu.VMEM((own.shape[0] // 128, 128, 128), jnp.bfloat16),
            pltpu.VMEM((row_tiles + 1, 128, 128), jnp.float32),
        ],
        out_shape=out_shape,
        compiler_params=grant(4 * (row_tiles + 5) * 128**2, [tiles, own, *out_shape]),
        cost_estimate=effort(slots),
    )(codes, counts, tiles, own)


def middle_sweep(codes, counts, tiles, sums, pieces, shard):
    smem, slots = pl.BlockSpec(memory_space=pltpu.SMEM), tiles.shape[0]
    panel = shard + sum(p.shape[0] for p in pieces) // 128
    return pl.pallas_call(
        functools.partial(middle_kernel, shard=shard),
        in_specs=[smem] * 2 + [VMEM] * (2 + len(pieces)),
        out_specs=VMEM,
        scratch_shapes=[pltpu.VMEM((panel, 128, 128), jnp.bfloat16)],
        out_shape=jax.ShapeDtypeStruct(sums.shape, jnp.float32),
        compiler_params=grant(2 * panel * 128**2, [tiles, sums, sums, *pieces]),
        cost_estimate=effort(slots),
    )(codes, counts, tiles, sums, *pieces)


def late_kernel(codes, counts, tiles_ref, sums_ref, weights_ref, *refs, shard):
    count_out = weights_ref.shape[0] // shard
    piece_refs, out_refs, (panel, acc) = refs[: -2 - count_out], refs[-2 - count_out : -2], refs[-2:]
    fill_panel(panel, piece_refs)

    def begin(n, carry):
        acc[n] = sums_ref[n]
        return carry

    lax.fori_loop(0, weights_ref.shape[0], begin, 0)

    def multiply(slot, col, row):
        part = panel[col & (panel.shape[0] - 1)]
        acc[row] += jnp.dot(tiles_ref[slot], part, preferred_element_type=jnp.float32)

    walk(codes, counts, [2], multiply)
    for n, target in enumerate(out_refs):
        tops = []
        for t in range(shard):
            target[t * 128 : (t + 1) * 128, :] = acc[n * shard + t].astype(jnp.bfloat16)
            tops.append(jnp.sum(weights_ref[n * shard + t], axis=0, keepdims=True))
        target[shard * 128 :, :] = split_half(jnp.concatenate(tops, axis=0))


def late_sweep(codes, counts, tiles, sums, weights, pieces, shard):
    smem, slots, row_tiles = pl.BlockSpec(memory_space=pltpu.SMEM), tiles.shape[0], weights.shape[0]
    rows = shard * 130
    out_shape = [jax.ShapeDtypeStruct((rows, 128), jnp.bfloat16)] * (row_tiles // shard)
    scratch = 4 * (row_tiles + 1) * 128**2 + sum(p.size for p in pieces) * 2
    return pl.pallas_call(
        functools.partial(late_kernel, shard=shard),
        in_specs=[smem] * 2 + [VMEM] * (3 + len(pieces)),
        out_specs=[VMEM] * len(out_shape),
        scratch_shapes=[
            pltpu.VMEM((sum(p.shape[0] for p in pieces) // 128, 128, 128), jnp.bfloat16),
            pltpu.VMEM((row_tiles + 1, 128, 128), jnp.float32),
        ],
        out_shape=out_shape,
        compiler_params=grant(scratch, [tiles, sums, weights, *pieces, *out_shape]),
        cost_estimate=effort(slots),
    )(codes, counts, tiles, sums, weights, *pieces)


def reverse_kernel(codes, counts, tiles_ref, *refs, pieces, lists, first, shard):
    piece_refs, out_refs, (panel, acc, mass) = refs[:pieces], refs[pieces:-3], refs[-3:]
    fill_panel(panel, piece_refs)
    clear(acc, mass)

    def multiply(slot, col, row):
        tile, part = tiles_ref[slot], panel[row & (panel.shape[0] - 1)]
        acc[col - first] += jnp.dot(part, tile, preferred_element_type=jnp.float32)
        mass[col - first] += fold_rows(tile.astype(jnp.float32))

    walk(codes, counts, lists, multiply)
    for n, target in enumerate(out_refs):
        tops = []
        for t in range(shard):
            target[t * 128 : (t + 1) * 128, :] = acc[n * shard + t].astype(jnp.bfloat16)
            tops.append(jnp.sum(mass[n * shard + t], axis=0, keepdims=True))
        target[shard * 128 :, :] = split_half(jnp.concatenate(tops, axis=0))


def reverse_sweep(codes, counts, lists, first, tiles, pieces, col_tiles, shard):
    smem, slots = pl.BlockSpec(memory_space=pltpu.SMEM), tiles.shape[0]
    out_shape = [jax.ShapeDtypeStruct((shard * 130, 128), jnp.bfloat16)] * (col_tiles // shard)
    scratch = 4 * (col_tiles + 1) * 136 * 128 + sum(p.size for p in pieces) * 2
    return pl.pallas_call(
        functools.partial(
            reverse_kernel,
            pieces=len(pieces),
            lists=lists,
            first=first,
            shard=shard,
        ),
        in_specs=[smem] * 2 + [VMEM] * (1 + len(pieces)),
        out_specs=[VMEM] * len(out_shape),
        scratch_shapes=[
            pltpu.VMEM((sum(p.shape[0] for p in pieces) // 128, 128, 128), jnp.bfloat16),
            pltpu.VMEM((col_tiles + 1, 128, 128), jnp.float32),
            pltpu.VMEM((col_tiles + 1, 8, 128), jnp.float32),
        ],
        out_shape=out_shape,
        compiler_params=grant(scratch, [tiles, *pieces, *out_shape]),
        cost_estimate=effort(slots),
    )(codes, counts, tiles, *pieces)


def pair_sum_kernel(keep_ref, got_ref, out_ref, *, body_rows):
    total = keep_ref[:body_rows].astype(jnp.float32) + got_ref[:body_rows].astype(jnp.float32)
    out_ref[:body_rows, :] = total.astype(out_ref.dtype)
    mass = both_halves(keep_ref[body_rows:]) + both_halves(got_ref[body_rows:])
    if out_ref.dtype == jnp.float32:
        out_ref[body_rows:, :] = jnp.concatenate([mass, jnp.zeros_like(mass)], axis=0)
    else:
        out_ref[body_rows:, :] = split_half(mass)


def both_halves(block):
    wide = block.astype(jnp.float32)
    half = wide.shape[0] // 2
    return wide[:half] + wide[half:]


def pair_sum(keep, got, body_rows, kind):
    return pl.pallas_call(
        functools.partial(pair_sum_kernel, body_rows=body_rows),
        out_shape=jax.ShapeDtypeStruct(keep.shape, kind),
        in_specs=[VMEM] * 2,
        out_specs=VMEM,
        compiler_params=params(48),
    )(keep, got)


def mix(total, scale, seeds, t):
    classes = lax.broadcasted_iota(jnp.int32, (128, 128), 0)
    labels = jnp.where(classes == seeds[t : t + 1, :], 1.0 - BLEND, 0.0)
    return total * scale[t : t + 1, :] + labels


def audio_kernel(seed_ref, own_ref, *refs, shard):
    got, (half_ref, turned_ref) = refs[:-2], refs[-2:]
    body = shard * 128
    mass = own_ref[body : body + shard, :]
    for g in got:
        mass += both_halves(g[body:])
    scale = BLEND / jnp.sqrt(mass)
    seeds = seed_ref[...]
    for t in range(shard):
        span = slice(t * 128, (t + 1) * 128)
        total = own_ref[span, :]
        for g in got:
            total += g[span, :].astype(jnp.float32)
        scores = mix(total.T, scale, seeds, t)
        turned_ref[span, :] = scores
        half_ref[span, :] = scores.astype(jnp.bfloat16)


def audio_blend(seeds, own, got):
    shard = seeds.shape[0]
    shape = (shard * 128, 128)
    return pl.pallas_call(
        functools.partial(audio_kernel, shard=shard),
        out_shape=[
            jax.ShapeDtypeStruct(shape, jnp.bfloat16),
            jax.ShapeDtypeStruct(shape, jnp.float32),
        ],
        in_specs=[VMEM] * (2 + len(got)),
        out_specs=[VMEM] * 2,
        compiler_params=params(48),
    )(seeds, own, *got)


def flip_kernel(turned_ref, out_ref):
    for t in range(out_ref.shape[0] // 128):
        span = slice(t * 128, (t + 1) * 128)
        out_ref[span, :] = turned_ref[span, :].T


def flip(turned):
    return pl.pallas_call(
        flip_kernel,
        out_shape=jax.ShapeDtypeStruct(turned.shape, jnp.float32),
        in_specs=[VMEM],
        out_specs=VMEM,
        compiler_params=params(48),
    )(turned)


def video_kernel(seed_ref, *refs, shard):
    got, out_ref = refs[:-1], refs[-1]
    body = shard * 128
    scale = BLEND / jnp.sqrt(sum(both_halves(r[body:]) for r in got))
    seeds = seed_ref[...]
    for t in range(shard):
        span = slice(t * 128, (t + 1) * 128)
        total = sum(r[span, :].astype(jnp.float32) for r in got)
        out_ref[span, :] = mix(total, scale, seeds, t).T


def video_blend(seeds, pieces):
    shard = seeds.shape[0]
    return pl.pallas_call(
        functools.partial(video_kernel, shard=shard),
        out_shape=jax.ShapeDtypeStruct((shard * 128, 128), jnp.float32),
        in_specs=[VMEM] * (1 + len(pieces)),
        out_specs=VMEM,
        compiler_params=params(48),
    )(seeds, *pieces)


def partner(value, axis, mask):
    size = lax.axis_size(axis)
    return lax.ppermute(value, axis, [(i, i ^ mask) for i in range(size)])


def body(video_scores_in, audio_seed, video_seed, tile_values, tile_rows, tile_cols, tile_count):
    tiles = tile_values[0, 0]
    shard = video_scores_in.shape[0] // 128
    n_row, n_col = lax.axis_size("row"), lax.axis_size("col")
    row_tiles, col_tiles = n_col * shard, n_row * shard
    audio_seeds = audio_seed.reshape(shard, 128)
    video_seeds = video_seed.reshape(shard, 128)

    own = prep(video_scores_in)
    others = [partner(own, "row", m) for m in range(1, n_row)]
    codes, counts = plan(tile_rows, tile_cols, tile_count, tiles, col_tiles, shard)
    sums, weights = early_sweep(codes, counts, tiles, own, row_tiles)
    near, far = others[: n_row // 2 - 1], others[n_row // 2 - 1 :]
    sums = middle_sweep(codes, counts, tiles, sums, near, shard)
    payloads = late_sweep(codes, counts, tiles, sums, weights, far, shard)
    owned = {}
    for n in [*range(2, n_col, 2), 0]:
        kind = jnp.bfloat16 if n else jnp.float32
        got = partner(payloads[n + 1], "col", 1)
        owned[n] = pair_sum(payloads[n], got, shard * 128, kind)
    arrived = [partner(owned[n], "col", n) for n in range(n_col - 2, 0, -2)]
    half, turned = audio_blend(audio_seeds, owned[0], arrived)

    mine = [half] + [partner(half, "col", m) for m in range(2, n_col, 2)]
    pieces = [q for p in mine for q in (p, partner(p, "col", 1))]
    half_tiles = col_tiles // 2
    far = reverse_sweep(codes, counts, [2], half_tiles, tiles, pieces, half_tiles, shard)
    near = reverse_sweep(codes, counts, [0, 1], 0, tiles, pieces, half_tiles, shard)
    sums = list(near) + list(far)
    results = [sums[0]] + [partner(sums[m], "row", m) for m in range(1, n_row)]
    return flip(turned), video_blend(video_seeds, results)


def solution(mesh):
    in_specs = (
        P(("col", "row"), None),
        P(("row", "col")),
        P(("col", "row")),
        P("row", "col", None, None, None),
        P("row", "col", None),
        P("row", "col", None),
        P("row", "col"),
    )
    out_specs = (P(("row", "col"), None), P(("col", "row"), None))
    return jax.shard_map(body, mesh=mesh, in_specs=in_specs, out_specs=out_specs, check_vma=False)
```

```python
import functools

import jax
import jax.numpy as jnp
from jax import lax
from jax.experimental import pallas as pl
from jax.experimental.pallas import tpu as pltpu
from jax.sharding import PartitionSpec as P

BLEND = 0.75
GROUP = 32
PLACE = 8
VMEM = pl.BlockSpec(memory_space=pltpu.VMEM)


def params(mib):
    return pltpu.CompilerParams(vmem_limit_bytes=mib * 2**20)


def split_half(mass):
    high = mass.astype(jnp.bfloat16)
    low = (mass - high.astype(jnp.float32)).astype(jnp.bfloat16)
    return jnp.concatenate([high.astype(jnp.float32), low.astype(jnp.float32)], axis=0).astype(
        jnp.bfloat16
    )


def prep_kernel(video_ref, out_ref):
    out_ref[...] = video_ref[...].astype(jnp.bfloat16)


def prep(video):
    return pl.pallas_call(
        prep_kernel,
        out_shape=jax.ShapeDtypeStruct(video.shape, jnp.bfloat16),
        in_specs=[VMEM],
        out_specs=VMEM,
        compiler_params=params(48),
    )(video)


def plan_kernel(rows, cols, live_ref, _, codes_ref, counts, *, cap, half, shard):
    row_mask, col_mask = lax.axis_index("row") * shard, lax.axis_index("col") * shard
    live = live_ref[0, 0]
    for n in range(4):
        counts[n] = 0

    def place(block, carry):
        base = block * PLACE
        found = [(rows[0, 0, base + k], cols[0, 0, base + k]) for k in range(PLACE)]
        for k, (row, col) in enumerate(found):
            slot = base + k
            row, col = row ^ col_mask, col ^ row_mask
            region = (col >= shard).astype(jnp.int32) + (col >= half).astype(jnp.int32)
            region = jnp.where(slot < live, region, 3)
            count = counts[region]
            codes_ref[region * cap + count] = slot | (col << 12) | (row << 20)
            counts[region] = count + 1
        return carry

    lax.fori_loop(0, lax.div(live + (PLACE - 1), PLACE), place, 0)
    found = [counts[n] for n in range(3)]
    row_dummy = (lax.axis_size("col") * shard) << 20
    for n, count in enumerate(found):
        dummy = row_dummy | ((half if n < 2 else 2 * half) << 12)

        def pad(k, carry):
            codes_ref[n * cap + count + k] = dummy
            return carry

        lax.fori_loop(0, GROUP, pad, 0)


def plan(rows, cols, live, tiles, col_tiles, shard):
    cap = rows.shape[2] + GROUP
    smem = pl.BlockSpec(memory_space=pltpu.SMEM)
    return pl.pallas_call(
        functools.partial(plan_kernel, cap=cap, half=col_tiles // 2, shard=shard),
        out_shape=[
            jax.ShapeDtypeStruct((3 * cap + 128,), jnp.int32),
            jax.ShapeDtypeStruct((4,), jnp.int32),
        ],
        in_specs=[smem] * 3 + [VMEM],
        out_specs=[smem] * 2,
        compiler_params=grant(0, [tiles]),
    )(rows, cols, live, tiles)


def walk(codes, counts, lists, visit):
    cap = (codes.shape[0] - 128) // 3
    for n in lists:

        def group(start, size):
            for k in range(size):
                code = codes[n * cap + start + k]
                col = lax.shift_right_logical(code, 12) & 0xFF
                visit(code & 0xFFF, col, lax.shift_right_logical(code, 20))

        def whole(g, carry):
            group(g * GROUP, GROUP)
            return carry

        full = lax.div(counts[n] + (GROUP // 2 - 1), GROUP)
        lax.fori_loop(0, full, whole, 0)
        pl.when(counts[n] > full * GROUP)(lambda: group(full * GROUP, GROUP // 2))


def fill_panel(panel, piece_refs):
    tiles = piece_refs[0].shape[0] // 128
    for m, piece in enumerate(piece_refs):
        for t in range(tiles):
            panel[m * tiles + t] = piece[t * 128 : (t + 1) * 128, :]


def clear(*sums):
    def one(n, carry):
        for ref in sums:
            ref[n] = jnp.zeros(ref.shape[1:], jnp.float32)
        return carry

    lax.fori_loop(0, sums[0].shape[0] - 1, one, 0)


def fold_rows(tile):
    return jnp.sum(tile.reshape(16, 8, 128), axis=0)


def early_kernel(codes, counts, tiles_ref, own_ref, sums_ref, weights_ref, panel, mass):
    fill_panel(panel, [own_ref])
    clear(mass)
    ones = jnp.ones((128, 128), jnp.bfloat16)

    def begin(n, carry):
        sums_ref[n] = jnp.zeros((128, 128), jnp.float32)
        return carry

    def multiply(slot, col, row):
        part = panel[col & (panel.shape[0] - 1)]
        sums_ref[row] += jnp.dot(tiles_ref[slot], part, preferred_element_type=jnp.float32)

    def weigh(slot, col, row):
        mass[row] += jnp.dot(tiles_ref[slot], ones, preferred_element_type=jnp.float32)

    lax.fori_loop(0, sums_ref.shape[0], begin, 0)
    walk(codes, counts, [0], multiply)
    walk(codes, counts, [0, 1, 2], weigh)

    diagonal = lax.broadcasted_iota(jnp.int32, (128, 128), 0) == lax.broadcasted_iota(
        jnp.int32, (128, 128), 1
    )

    def hand(n, carry):
        weights_ref[n] = fold_rows(jnp.where(diagonal, mass[n], 0.0))
        return carry

    lax.fori_loop(0, weights_ref.shape[0], hand, 0)


def middle_kernel(codes, counts, tiles_ref, sums_ref, *refs, shard):
    *piece_refs, out_ref, panel = refs
    fill_panel(panel.at[pl.ds(shard, panel.shape[0] - shard)], piece_refs)
    panel[0] = jnp.zeros((128, 128), jnp.bfloat16)

    def begin(n, carry):
        out_ref[n] = sums_ref[n]
        return carry

    def multiply(slot, col, row):
        part = panel[col & (panel.shape[0] - 1)]
        out_ref[row] += jnp.dot(tiles_ref[slot], part, preferred_element_type=jnp.float32)

    lax.fori_loop(0, sums_ref.shape[0], begin, 0)
    walk(codes, counts, [1], multiply)


def grant(scratch, arrays):
    size = sum(x.size * x.dtype.itemsize for x in arrays)
    return params((scratch + (size if size > 24 * 2**20 else 0)) // 2**20 + 5)


def effort(slots):
    average = slots // 4
    return pl.CostEstimate(
        flops=16 * average * 128**3, bytes_accessed=average * 128 * 256, transcendentals=0
    )


def early_sweep(codes, counts, tiles, own, row_tiles):
    smem, slots = pl.BlockSpec(memory_space=pltpu.SMEM), tiles.shape[0]
    out_shape = [
        jax.ShapeDtypeStruct((row_tiles + 1, 128, 128), jnp.float32),
        jax.ShapeDtypeStruct((row_tiles, 8, 128), jnp.float32),
    ]
    return pl.pallas_call(
        early_kernel,
        in_specs=[smem] * 2 + [VMEM] * 2,
        out_specs=[VMEM] * 2,
        scratch_shapes=[
            pltpu.VMEM((own.shape[0] // 128, 128, 128), jnp.bfloat16),
            pltpu.VMEM((row_tiles + 1, 128, 128), jnp.float32),
        ],
        out_shape=out_shape,
        compiler_params=grant(4 * (row_tiles + 5) * 128**2, [tiles, own, *out_shape]),
        cost_estimate=effort(slots),
    )(codes, counts, tiles, own)


def middle_sweep(codes, counts, tiles, sums, pieces, shard):
    smem, slots = pl.BlockSpec(memory_space=pltpu.SMEM), tiles.shape[0]
    panel = shard + sum(p.shape[0] for p in pieces) // 128
    return pl.pallas_call(
        functools.partial(middle_kernel, shard=shard),
        in_specs=[smem] * 2 + [VMEM] * (2 + len(pieces)),
        out_specs=VMEM,
        scratch_shapes=[pltpu.VMEM((panel, 128, 128), jnp.bfloat16)],
        out_shape=jax.ShapeDtypeStruct(sums.shape, jnp.float32),
        compiler_params=grant(2 * panel * 128**2, [tiles, sums, sums, *pieces]),
        cost_estimate=effort(slots),
    )(codes, counts, tiles, sums, *pieces)


def late_kernel(codes, counts, tiles_ref, sums_ref, weights_ref, *refs, shard):
    count_out = weights_ref.shape[0] // shard
    piece_refs, out_refs, (panel, acc) = refs[: -2 - count_out], refs[-2 - count_out : -2], refs[-2:]
    fill_panel(panel, piece_refs)

    def begin(n, carry):
        acc[n] = sums_ref[n]
        return carry

    lax.fori_loop(0, weights_ref.shape[0], begin, 0)

    def multiply(slot, col, row):
        part = panel[col & (panel.shape[0] - 1)]
        acc[row] += jnp.dot(tiles_ref[slot], part, preferred_element_type=jnp.float32)

    walk(codes, counts, [2], multiply)
    for n, target in enumerate(out_refs):
        tops = []
        for t in range(shard):
            target[t * 128 : (t + 1) * 128, :] = acc[n * shard + t].astype(jnp.bfloat16)
            tops.append(jnp.sum(weights_ref[n * shard + t], axis=0, keepdims=True))
        target[shard * 128 :, :] = split_half(jnp.concatenate(tops, axis=0))


def late_sweep(codes, counts, tiles, sums, weights, pieces, shard):
    smem, slots, row_tiles = pl.BlockSpec(memory_space=pltpu.SMEM), tiles.shape[0], weights.shape[0]
    rows = shard * 130
    out_shape = [jax.ShapeDtypeStruct((rows, 128), jnp.bfloat16)] * (row_tiles // shard)
    scratch = 4 * (row_tiles + 1) * 128**2 + sum(p.size for p in pieces) * 2
    return pl.pallas_call(
        functools.partial(late_kernel, shard=shard),
        in_specs=[smem] * 2 + [VMEM] * (3 + len(pieces)),
        out_specs=[VMEM] * len(out_shape),
        scratch_shapes=[
            pltpu.VMEM((sum(p.shape[0] for p in pieces) // 128, 128, 128), jnp.bfloat16),
            pltpu.VMEM((row_tiles + 1, 128, 128), jnp.float32),
        ],
        out_shape=out_shape,
        compiler_params=grant(scratch, [tiles, sums, weights, *pieces, *out_shape]),
        cost_estimate=effort(slots),
    )(codes, counts, tiles, sums, weights, *pieces)


def reverse_kernel(codes, counts, tiles_ref, *refs, pieces, lists, first, shard):
    piece_refs, out_refs, (panel, acc, mass) = refs[:pieces], refs[pieces:-3], refs[-3:]
    fill_panel(panel, piece_refs)
    clear(acc, mass)

    def multiply(slot, col, row):
        tile, part = tiles_ref[slot], panel[row & (panel.shape[0] - 1)]
        acc[col - first] += jnp.dot(part, tile, preferred_element_type=jnp.float32)
        mass[col - first] += fold_rows(tile.astype(jnp.float32))

    walk(codes, counts, lists, multiply)
    for n, target in enumerate(out_refs):
        tops = []
        for t in range(shard):
            target[t * 128 : (t + 1) * 128, :] = acc[n * shard + t].astype(jnp.bfloat16)
            tops.append(jnp.sum(mass[n * shard + t], axis=0, keepdims=True))
        target[shard * 128 :, :] = split_half(jnp.concatenate(tops, axis=0))


def reverse_sweep(codes, counts, lists, first, tiles, pieces, col_tiles, shard):
    smem, slots = pl.BlockSpec(memory_space=pltpu.SMEM), tiles.shape[0]
    out_shape = [jax.ShapeDtypeStruct((shard * 130, 128), jnp.bfloat16)] * (col_tiles // shard)
    scratch = 4 * (col_tiles + 1) * 136 * 128 + sum(p.size for p in pieces) * 2
    return pl.pallas_call(
        functools.partial(
            reverse_kernel,
            pieces=len(pieces),
            lists=lists,
            first=first,
            shard=shard,
        ),
        in_specs=[smem] * 2 + [VMEM] * (1 + len(pieces)),
        out_specs=[VMEM] * len(out_shape),
        scratch_shapes=[
            pltpu.VMEM((sum(p.shape[0] for p in pieces) // 128, 128, 128), jnp.bfloat16),
            pltpu.VMEM((col_tiles + 1, 128, 128), jnp.float32),
            pltpu.VMEM((col_tiles + 1, 8, 128), jnp.float32),
        ],
        out_shape=out_shape,
        compiler_params=grant(scratch, [tiles, *pieces, *out_shape]),
        cost_estimate=effort(slots),
    )(codes, counts, tiles, *pieces)


def pair_sum_kernel(keep_ref, got_ref, out_ref, *, body_rows):
    total = keep_ref[:body_rows].astype(jnp.float32) + got_ref[:body_rows].astype(jnp.float32)
    out_ref[:body_rows, :] = total.astype(out_ref.dtype)
    mass = both_halves(keep_ref[body_rows:]) + both_halves(got_ref[body_rows:])
    if out_ref.dtype == jnp.float32:
        out_ref[body_rows:, :] = jnp.concatenate([mass, jnp.zeros_like(mass)], axis=0)
    else:
        out_ref[body_rows:, :] = split_half(mass)


def both_halves(block):
    wide = block.astype(jnp.float32)
    half = wide.shape[0] // 2
    return wide[:half] + wide[half:]


def pair_sum(keep, got, body_rows, kind):
    return pl.pallas_call(
        functools.partial(pair_sum_kernel, body_rows=body_rows),
        out_shape=jax.ShapeDtypeStruct(keep.shape, kind),
        in_specs=[VMEM] * 2,
        out_specs=VMEM,
        compiler_params=params(48),
    )(keep, got)


def mix(total, scale, seeds, t):
    classes = lax.broadcasted_iota(jnp.int32, (128, 128), 0)
    labels = jnp.where(classes == seeds[t : t + 1, :], 1.0 - BLEND, 0.0)
    return total * scale[t : t + 1, :] + labels


def audio_kernel(seed_ref, own_ref, *refs, shard):
    got, (half_ref, turned_ref) = refs[:-2], refs[-2:]
    body = shard * 128
    mass = own_ref[body : body + shard, :]
    for g in got:
        mass += both_halves(g[body:])
    scale = BLEND / jnp.sqrt(mass)
    seeds = seed_ref[...]
    for t in range(shard):
        span = slice(t * 128, (t + 1) * 128)
        total = own_ref[span, :]
        for g in got:
            total += g[span, :].astype(jnp.float32)
        scores = mix(total.T, scale, seeds, t)
        turned_ref[span, :] = scores
        half_ref[span, :] = scores.astype(jnp.bfloat16)


def audio_blend(seeds, own, got):
    shard = seeds.shape[0]
    shape = (shard * 128, 128)
    return pl.pallas_call(
        functools.partial(audio_kernel, shard=shard),
        out_shape=[
            jax.ShapeDtypeStruct(shape, jnp.bfloat16),
            jax.ShapeDtypeStruct(shape, jnp.float32),
        ],
        in_specs=[VMEM] * (2 + len(got)),
        out_specs=[VMEM] * 2,
        compiler_params=params(48),
    )(seeds, own, *got)


def flip_kernel(turned_ref, out_ref):
    for t in range(out_ref.shape[0] // 128):
        span = slice(t * 128, (t + 1) * 128)
        out_ref[span, :] = turned_ref[span, :].T


def flip(turned):
    return pl.pallas_call(
        flip_kernel,
        out_shape=jax.ShapeDtypeStruct(turned.shape, jnp.float32),
        in_specs=[VMEM],
        out_specs=VMEM,
        compiler_params=params(48),
    )(turned)


def video_kernel(seed_ref, *refs, shard):
    got, out_ref = refs[:-1], refs[-1]
    body = shard * 128
    scale = BLEND / jnp.sqrt(sum(both_halves(r[body:]) for r in got))
    seeds = seed_ref[...]
    for t in range(shard):
        span = slice(t * 128, (t + 1) * 128)
        total = sum(r[span, :].astype(jnp.float32) for r in got)
        out_ref[span, :] = mix(total, scale, seeds, t).T


def video_blend(seeds, pieces):
    shard = seeds.shape[0]
    return pl.pallas_call(
        functools.partial(video_kernel, shard=shard),
        out_shape=jax.ShapeDtypeStruct((shard * 128, 128), jnp.float32),
        in_specs=[VMEM] * (1 + len(pieces)),
        out_specs=VMEM,
        compiler_params=params(48),
    )(seeds, *pieces)


def partner(value, axis, mask):
    size = lax.axis_size(axis)
    return lax.ppermute(value, axis, [(i, i ^ mask) for i in range(size)])


def body(video_scores_in, audio_seed, video_seed, tile_values, tile_rows, tile_cols, tile_count):
    tiles = tile_values[0, 0]
    shard = video_scores_in.shape[0] // 128
    n_row, n_col = lax.axis_size("row"), lax.axis_size("col")
    row_tiles, col_tiles = n_col * shard, n_row * shard
    audio_seeds = audio_seed.reshape(shard, 128)
    video_seeds = video_seed.reshape(shard, 128)

    own = prep(video_scores_in)
    others = [partner(own, "row", m) for m in range(1, n_row)]
    codes, counts = plan(tile_rows, tile_cols, tile_count, tiles, col_tiles, shard)
    sums, weights = early_sweep(codes, counts, tiles, own, row_tiles)
    near, far = others[: n_row // 2 - 1], others[n_row // 2 - 1 :]
    sums = middle_sweep(codes, counts, tiles, sums, near, shard)
    payloads = late_sweep(codes, counts, tiles, sums, weights, far, shard)
    owned = {}
    for n in [*range(2, n_col, 2), 0]:
        kind = jnp.bfloat16 if n else jnp.float32
        got = partner(payloads[n + 1], "col", 1)
        owned[n] = pair_sum(payloads[n], got, shard * 128, kind)
    arrived = [partner(owned[n], "col", n) for n in range(n_col - 2, 0, -2)]
    half, turned = audio_blend(audio_seeds, owned[0], arrived)

    mine = [half] + [partner(half, "col", m) for m in range(2, n_col, 2)]
    pieces = [q for p in mine for q in (p, partner(p, "col", 1))]
    half_tiles = col_tiles // 2
    far = reverse_sweep(codes, counts, [2], half_tiles, tiles, pieces, half_tiles, shard)
    near = reverse_sweep(codes, counts, [0, 1], 0, tiles, pieces, half_tiles, shard)
    sums = list(near) + list(far)
    results = [sums[0]] + [partner(sums[m], "row", m) for m in range(1, n_row)]
    return flip(turned), video_blend(video_seeds, results)


def solution(mesh):
    in_specs = (
        P(("col", "row"), None),
        P(("row", "col")),
        P(("col", "row")),
        P("row", "col", None, None, None),
        P("row", "col", None),
        P("row", "col", None),
        P("row", "col"),
    )
    out_specs = (P(("row", "col"), None), P(("col", "row"), None))
    return jax.shard_map(body, mesh=mesh, in_specs=in_specs, out_specs=out_specs, check_vma=False)
```
